256 devices in a mesh: wide: 64 (over x, z, core), narrow: 4 (over y).
Axes of the slice: x: 4, y: 4, z: 8, core: 2. Of those that a mesh axis runs over, the one named last changes fastest.
Arguments:
- queries: bfloat16 [512, 1024], P(('wide', 'narrow')), may hold values from -16 to 16
- archive_keys: bfloat16 [196608, 1024], P(('wide', 'narrow')), may hold values from -6 to 6
- futures: bfloat16 [196608, 1024], P(('wide', 'narrow')), may hold values from -6 to 6
- counts: int32 [256], P(('wide', 'narrow')), may hold values from 256 to 768
- owners: int32 [512], replicated, may hold values from 0 to 511, each once
Outputs:
- forecast: bfloat16 [512, 1024], P(('wide', 'narrow'))
The draws below stay inside these ranges and needn't reach their ends.
Inputs may be any that keep to these rules, and one draw needn't show every extreme that they name: owners is a permutation of 0 to 511.
All inputs are finite; a program needn't handle non-finite values.
Results may differ from the reference program's by a relative error of at most 0.004.
Values may be sent and summed in bfloat16 or wider, within the bound.
A program may use at most 64 MiB of HBM per device.

```python
import jax
import jax.numpy as jnp
from jax import lax

D = 1024
ROWS_DEV = 768
ARCHIVE = 196608
NQ = 512


def draw_archive_keys(key, part):
    key = jax.random.fold_in(key, 5)
    values = jnp.clip(jax.random.normal(key, (ARCHIVE, D), jnp.float32), -6.0, 6.0)
    return values.astype(jnp.bfloat16)


def draw_queries(key, part):
    key = jax.random.fold_in(key, 7)
    values = jnp.clip(jax.random.normal(key, (NQ, D), jnp.float32), -6.0, 6.0)
    return values.astype(jnp.bfloat16)


def draw_counts(key, part):
    key = jax.random.fold_in(key, 3)
    shard_count = ARCHIVE // ROWS_DEV
    lowest = (ROWS_DEV + 2) // 3
    values = jax.random.randint(key, (shard_count,), lowest, ROWS_DEV + 1, jnp.int32)
    picks = jax.random.permutation(jax.random.fold_in(key, 1), shard_count)
    values = values.at[picks[0]].set(ROWS_DEV)
    values = values.at[picks[1]].set(lowest)
    return values


def steps_of(key, shape, split, low, largest):
    factor_of = 1.0
    for dim, shards_of in split:
        heights = jax.random.uniform(jax.random.fold_in(jax.random.fold_in(key, 6), dim), (shards_of,), jnp.float32, low / len(split), largest / len(split))
        factor_of = factor_of * jnp.repeat(jnp.exp(heights), shape[dim] // shards_of).reshape((-1,) + (1,) * (len(shape) - 1 - dim))
    return factor_of


def scatter_about(stream_key, shape, width, most, split=(), held_as=jnp.bfloat16):
    factor_of = steps_of(stream_key, shape, split, -0.22, 0.18) if split else 1.0
    values = jax.random.normal(stream_key, shape, jnp.float32) * width * factor_of
    return jnp.minimum(jnp.maximum(values, -most), most).astype(held_as)


def setup_inputs(seed: int = 0) -> dict:
    splits = jax.random.split(jax.random.key(seed), 6)
    queries = draw_queries(jax.random.fold_in(splits[5], 71), 0)
    archive_keys = draw_archive_keys(jax.random.fold_in(splits[5], 71), 0)
    futures = scatter_about(splits[2], (ARCHIVE, D), 1.0, 6.0, ((0, 256),))
    counts = draw_counts(jax.random.fold_in(splits[5], 71), 0)
    owners = jax.random.permutation(splits[4], NQ).astype(jnp.int32)
    return {"queries": queries, "archive_keys": archive_keys, "futures": futures, "counts": counts, "owners": owners}


score_scale = 3.0

def reference(queries, archive_keys, futures, counts, owners):
    shard_count = ARCHIVE // ROWS_DEV
    key_blocks = archive_keys.reshape(shard_count, ROWS_DEV, D)
    value_blocks = futures.reshape(shard_count, ROWS_DEV, D)
    row_index = jnp.arange(ROWS_DEV, dtype=jnp.int32)
    score_factor = score_scale / D ** 0.5

    def shard_scores(packed):
        block, valid_count = packed
        scores = jnp.dot(queries, block.T, preferred_element_type=jnp.float32) * score_factor
        return jnp.where(row_index[None, :] < valid_count, scores, -jnp.inf)
    all_scores = lax.map(shard_scores, (key_blocks, counts))
    maxima = lax.optimization_barrier(jnp.max(lax.optimization_barrier(jnp.max(all_scores, axis=2)), axis=0))

    def accumulate(carry, packed):
        numer, denom = carry
        scores, block, valid_count = packed
        kernel = jnp.where(row_index[None, :] < valid_count, jnp.exp(scores - maxima[:, None]), 0.0)
        numer = numer + jnp.dot(kernel.astype(jnp.bfloat16), block, preferred_element_type=jnp.float32)
        denom = denom + lax.optimization_barrier(jnp.sum(kernel, axis=1))
        return ((numer, denom), None)
    start = (jnp.zeros((NQ, D), jnp.float32), jnp.zeros((NQ,), jnp.float32))
    (numer, denom), _ = lax.scan(accumulate, start, (all_scores, value_blocks, counts))
    analog = numer[owners] / denom[owners][:, None]
    norm_factor = lax.rsqrt(lax.optimization_barrier(jnp.mean(analog * analog, axis=1, keepdims=True)) + 1e-06)
    return (analog * norm_factor).astype(jnp.bfloat16)
```

```python
import jax
import jax.numpy as jnp
from jax import lax
from jax.experimental import pallas as pl
from jax.experimental.pallas import tpu as pltpu
from jax.sharding import PartitionSpec as P

MESH = pl.DeviceIdType.MESH

NX, NY, NZ = 4, 4, 8
PLANE = NX * NY
ROWS = 2 * NZ
MINE = PLANE * ROWS
WIDTH = 1024
HALF = 512
STATS = 128
ARCHIVE = 768
TILE = 256

score_scale = 3.0
exponent_factor = score_scale / 32.0 * 1.4426950408889634


def natural_row(core, position):
    x, y = position // 64, (position // 16) % 4
    z, row = (position // 2) % 8, position % 2
    return x * 128 + z * 16 + core * 8 + y * 2 + row


def kernel(
    queries,
    keys_hbm,
    futures_hbm,
    counts,
    owners,
    out,
    zgather,
    gather32,
    gathered,
    keys,
    futures,
    limits,
    onehot,
    scores,
    weights,
    part_send,
    part_recv,
    zpart_send,
    zpart_recv,
    local_sem,
    archive_send,
    archive_recv,
    zg_send,
    zg_recv,
    pg_send,
    pg_recv,
    fw_send,
    fw_recv,
    ps_send,
    ps_recv,
    zs_send,
    zs_recv,
):
    wide, y = lax.axis_index("wide"), lax.axis_index("narrow")
    x, z, core = wide // 16, (wide // 2) % 8, wide % 2
    plane = x * NY + y

    def device(x, y, z, core):
        return {"wide": (x * NZ + z) * 2 + core, "narrow": y}

    def z_peer(step):
        other = (z + step) % NZ
        return other, device(x, y, other, core)

    def plane_peer(step):
        other_x, other_y = (x + step // NY) % NX, (y + step % NY) % NY
        return other_x * NY + other_y, device(other_x, other_y, z, core)

    twin = device(x, y, z, 1 - core)

    def remote(src, dst, send, recv, target):
        return pltpu.make_async_remote_copy(
            src_ref=src, dst_ref=dst, send_sem=send, recv_sem=recv, device_id=target, device_id_type=MESH
        )

    own_keys = pltpu.make_async_copy(keys_hbm, keys.at[0], local_sem.at[0])
    own_futures = pltpu.make_async_copy(futures_hbm, futures.at[0], local_sem.at[1])
    own_keys.start()
    own_futures.start()

    barrier = pltpu.get_barrier_semaphore()

    def greet_z(step, carry):
        pl.semaphore_signal(barrier, inc=1, device_id=z_peer(step)[1], device_id_type=MESH)
        return carry

    def greet_plane(step, carry):
        pl.semaphore_signal(barrier, inc=1, device_id=plane_peer(step)[1], device_id_type=MESH)
        return carry

    lax.fori_loop(1, NZ, greet_z, 0)
    lax.fori_loop(1, PLANE, greet_plane, 0)
    pl.semaphore_signal(barrier, inc=1, device_id=twin, device_id_type=MESH)
    zgather[z] = queries[...].astype(jnp.float32)
    limits[0] = jnp.full((8, 128), counts[0], jnp.int32).astype(jnp.float32)
    pl.semaphore_wait(barrier, NZ - 1 + PLANE - 1 + 1)

    def zg_copy(step):
        other, target = z_peer(step)
        return remote(zgather.at[z], zgather.at[z], zg_send.at[step], zg_recv.at[z], target)

    def zg_start(step, carry):
        zg_copy(step).start()
        return carry

    lax.fori_loop(1, NZ, zg_start, 0)

    to_twin = (
        remote(limits.at[0], limits.at[1], archive_send.at[2], archive_recv.at[2], twin),
        remote(keys_hbm, keys.at[1], archive_send.at[0], archive_recv.at[0], twin),
        remote(futures_hbm, futures.at[1], archive_send.at[1], archive_recv.at[1], twin),
    )
    for copy in to_twin:
        copy.start()

    position = lax.broadcasted_iota(jnp.int32, (1, 2 * MINE), 1)
    held = natural_row(position // MINE, position % MINE)
    lane = lax.broadcasted_iota(jnp.int32, (64, 128), 1)
    wanted = natural_row(core, lax.broadcasted_iota(jnp.int32, (64, 128), 0))
    for block in range(NX):
        picked = jnp.where(lane == wanted, owners[block : block + 1, :].astype(jnp.float32), 0.0)
        owner = jnp.sum(picked, axis=1, keepdims=True)
        onehot[block * 64 : block * 64 + 64, :] = jnp.where(
            owner == held.astype(jnp.float32), 1.0, 0.0
        ).astype(jnp.bfloat16)

    def zg_wait(step, carry):
        other, target = z_peer(step)
        remote(zgather.at[other], zgather.at[other], zg_send.at[step], zg_recv.at[other], target).wait_recv()
        return carry

    lax.fori_loop(1, NZ, zg_wait, 0)
    for k in range(NZ):
        gather32[2 * k : 2 * k + 2, :] = zgather[k]
    gathered[core, plane] = gather32[...].astype(jnp.bfloat16)

    def pg_start(step, carry):
        other, target = plane_peer(step)
        block = gathered.at[core, plane]
        remote(block, block, pg_send.at[step], pg_recv.at[plane], target).start()
        return carry

    lax.fori_loop(1, PLANE, pg_start, 0)

    def fw_copy(other):
        block = gathered.at[core, other]
        return remote(block, block, fw_send.at[other], fw_recv.at[other], twin)

    fw_copy(plane).start()

    def pg_wait(step, carry):
        other, target = plane_peer(step)
        block = gathered.at[core, other]
        remote(block, block, pg_send.at[step], pg_recv.at[other], target).wait_recv()
        fw_copy(other).start()
        return carry

    lax.fori_loop(1, PLANE, pg_wait, 0)

    own_keys.wait()
    own_futures.wait()
    for copy in to_twin:
        copy.wait()

    def fw_wait(other, carry):
        block = gathered.at[1 - core, other]
        remote(block, block, fw_send.at[other], fw_recv.at[other], twin).wait_recv()
        return carry

    lax.fori_loop(0, PLANE, fw_wait, 0)

    every = gathered[...].reshape(2 * MINE, WIDTH)
    mine = jnp.dot(onehot[...], every, preferred_element_type=jnp.float32).astype(jnp.bfloat16)

    column = lax.broadcasted_iota(jnp.int32, (1, TILE), 1).astype(jnp.float32)
    best = None
    for half in range(2):
        limit = limits[half, 0:1, 0:1]
        for tile in range(ARCHIVE // TILE):
            part = lax.dot_general(
                mine,
                keys[half, tile * TILE : (tile + 1) * TILE, :],
                (((1,), (1,)), ((), ())),
                preferred_element_type=jnp.float32,
            )
            part = jnp.where(column + float(tile * TILE) < limit, part, -1e30)
            at = half * ARCHIVE + tile * TILE
            scores[:, at : at + TILE] = part
            top = jnp.max(part, axis=1, keepdims=True)
            best = top if best is None else jnp.maximum(best, top)
    best = best.astype(jnp.bfloat16).astype(jnp.float32)
    total = jnp.zeros((MINE, 1), jnp.float32)
    for tile in range(2 * ARCHIVE // TILE):
        span = slice(tile * TILE, (tile + 1) * TILE)
        weight = jnp.exp2((scores[:, span] - best) * exponent_factor)
        weights[:, span] = weight.astype(jnp.bfloat16)
        total = total + jnp.sum(weight, axis=1, keepdims=True)

    stat_lane = lax.broadcasted_iota(jnp.int32, (1, STATS), 1)
    high = total.astype(jnp.bfloat16).astype(jnp.float32)
    stats = jnp.where(stat_lane < 32, best, jnp.where(stat_lane < 64, high, total - high))
    part_send[:, :, WIDTH:] = stats.astype(jnp.bfloat16).reshape(PLANE, ROWS, STATS)
    for half in range(2):
        span = slice(half * HALF, (half + 1) * HALF)
        sums = None
        for side in range(2):
            term = jnp.dot(
                weights[:, side * ARCHIVE : (side + 1) * ARCHIVE],
                futures[side, :, span],
                preferred_element_type=jnp.float32,
            )
            sums = term if sums is None else sums + term
        part_send[:, :, span] = sums.astype(jnp.bfloat16).reshape(PLANE, ROWS, HALF)

    def ps_start(step, carry):
        other, target = plane_peer(step)
        remote(part_send.at[other], part_recv.at[plane], ps_send.at[step], ps_recv.at[plane], target).start()
        return carry

    lax.fori_loop(1, PLANE, ps_start, 0)
    part_recv[plane] = part_send[plane]

    def ps_wait(step, carry):
        other, target = plane_peer(step)
        remote(part_send.at[other], part_recv.at[other], ps_send.at[step], ps_recv.at[other], target).wait_recv()
        return carry

    lax.fori_loop(1, PLANE, ps_wait, 0)

    best = part_recv[0, :, WIDTH : WIDTH + 1].astype(jnp.float32)
    for k in range(1, PLANE):
        best = jnp.maximum(best, part_recv[k, :, WIDTH : WIDTH + 1].astype(jnp.float32))
    sums = jnp.zeros((ROWS, WIDTH), jnp.float32)
    total = jnp.zeros((ROWS, 1), jnp.float32)
    for k in range(PLANE):
        stats = part_recv[k, :, WIDTH:].astype(jnp.float32)
        scale = jnp.exp2((stats[:, 0:1] - best) * exponent_factor)
        sums = sums + part_recv[k, :, :WIDTH].astype(jnp.float32) * scale
        total = total + (stats[:, 32:33] + stats[:, 64:65]) * scale
    stats = jnp.where(stat_lane < 64, best, total)
    for k in range(NZ):
        zpart_send[k, :, :WIDTH] = sums[2 * k : 2 * k + 2, :]
        zpart_send[k, :, WIDTH:] = stats[2 * k : 2 * k + 2, :]

    def zs_start(step, carry):
        other, target = z_peer(step)
        remote(zpart_send.at[other], zpart_recv.at[z], zs_send.at[step], zs_recv.at[z], target).start()
        return carry

    lax.fori_loop(1, NZ, zs_start, 0)
    zpart_recv[z] = zpart_send[z]

    def zs_wait(step, carry):
        other, target = z_peer(step)
        remote(zpart_send.at[other], zpart_recv.at[other], zs_send.at[step], zs_recv.at[other], target).wait_recv()
        return carry

    lax.fori_loop(1, NZ, zs_wait, 0)

    best = zpart_recv[0, :, WIDTH : WIDTH + 1]
    for k in range(1, NZ):
        best = jnp.maximum(best, zpart_recv[k, :, WIDTH : WIDTH + 1])
    sums = jnp.zeros((2, WIDTH), jnp.float32)
    total = jnp.zeros((2, 1), jnp.float32)
    for k in range(NZ):
        stats = zpart_recv[k, :, WIDTH:]
        scale = jnp.exp2((stats[:, 0:1] - best) * exponent_factor)
        sums = sums + zpart_recv[k, :, :WIDTH] * scale
        total = total + stats[:, 64:65] * scale
    analog = sums / total
    norm_factor = lax.rsqrt(jnp.mean(analog * analog, axis=1, keepdims=True) + 1e-06)
    out[...] = (analog * norm_factor).astype(jnp.bfloat16)

    def z_sent(step, carry):
        other, target = z_peer(step)
        zg_copy(step).wait_send()
        remote(zpart_send.at[other], zpart_recv.at[z], zs_send.at[step], zs_recv.at[z], target).wait_send()
        return carry

    def plane_sent(step, carry):
        other, target = plane_peer(step)
        block = gathered.at[core, plane]
        remote(block, block, pg_send.at[step], pg_recv.at[plane], target).wait_send()
        remote(part_send.at[other], part_recv.at[plane], ps_send.at[step], ps_recv.at[plane], target).wait_send()
        return carry

    def fw_sent(other, carry):
        fw_copy(other).wait_send()
        return carry

    lax.fori_loop(1, NZ, z_sent, 0)
    lax.fori_loop(1, PLANE, plane_sent, 0)
    lax.fori_loop(0, PLANE, fw_sent, 0)


def body(queries, archive_keys, futures, counts, owners):
    vmem = pl.BlockSpec(memory_space=pltpu.VMEM)
    smem = pl.BlockSpec(memory_space=pltpu.SMEM)
    anywhere = pl.BlockSpec(memory_space=pl.ANY)
    dma = pltpu.SemaphoreType.DMA
    return pl.pallas_call(
        kernel,
        out_shape=jax.ShapeDtypeStruct((2, WIDTH), jnp.bfloat16),
        in_specs=[vmem, anywhere, anywhere, smem, vmem],
        out_specs=vmem,
        scratch_shapes=[
            pltpu.VMEM((NZ, 2, WIDTH), jnp.float32),
            pltpu.VMEM((ROWS, WIDTH), jnp.float32),
            pltpu.VMEM((2, PLANE, ROWS, WIDTH), jnp.bfloat16),
            pltpu.VMEM((2, ARCHIVE, WIDTH), jnp.bfloat16),
            pltpu.VMEM((2, ARCHIVE, WIDTH), jnp.bfloat16),
            pltpu.VMEM((2, 8, 128), jnp.float32),
            pltpu.VMEM((MINE, 2 * MINE), jnp.bfloat16),
            pltpu.VMEM((MINE, 2 * ARCHIVE), jnp.float32),
            pltpu.VMEM((MINE, 2 * ARCHIVE), jnp.bfloat16),
            pltpu.VMEM((PLANE, ROWS, WIDTH + STATS), jnp.bfloat16),
            pltpu.VMEM((PLANE, ROWS, WIDTH + STATS), jnp.bfloat16),
            pltpu.VMEM((NZ, 2, WIDTH + STATS), jnp.float32),
            pltpu.VMEM((NZ, 2, WIDTH + STATS), jnp.float32),
            dma((2,)),
            dma((3,)),
            dma((3,)),
            dma((NZ,)),
            dma((NZ,)),
            dma((PLANE,)),
            dma((PLANE,)),
            dma((PLANE,)),
            dma((PLANE,)),
            dma((PLANE,)),
            dma((PLANE,)),
            dma((NZ,)),
            dma((NZ,)),
        ],
        compiler_params=pltpu.CompilerParams(
            collective_id=0, has_side_effects=True, vmem_limit_bytes=40 * 2**20
        ),
        name="analog_forecast",
    )(queries, archive_keys, futures, counts, owners.reshape(4, 128))


def solution(mesh):
    rows = P(("wide", "narrow"), None)
    return jax.shard_map(
        body,
        mesh=mesh,
        in_specs=(rows, rows, rows, P(("wide", "narrow")), P()),
        out_specs=rows,
        check_vma=False,
    )
```

```python
import jax
import jax.numpy as jnp
from jax import lax
from jax.experimental import pallas as pl
from jax.experimental.pallas import tpu as pltpu
from jax.sharding import PartitionSpec as P

MESH = pl.DeviceIdType.MESH

NX, NY, NZ = 4, 4, 8
PLANE = NX * NY
ROWS = 16
MINE = PLANE * ROWS
GROUP = MINE // 2
WIDTH = 1024
HALF = 512
STATS = 128
ARCHIVE = 768
TILE = 256

NEAR, FAR = (0, 1, 7, 6), (4, 3, 5, 2)
OFFSETS = NEAR, FAR

STEPS = sorted(
    [(a, b) for a in range(NX) for b in range(NY) if a or b],
    key=lambda s: -(min(s[0], NX - s[0]) + min(s[1], NY - s[1])),
)

score_scale = 3.0
exponent_factor = score_scale / 32.0 * 1.4426950408889634


def pick(index, values):
    result = jnp.full_like(index, values[0])
    for k in range(1, len(values)):
        result = jnp.where(index == k, values[k], result)
    return result


def natural_row(x, y, z, core, row):
    return x * 128 + z * 16 + core * 8 + y * 2 + row


def kernel(
    queries_hbm,
    keys_hbm,
    futures_hbm,
    counts_hbm,
    owners_hbm,
    out,
    queries,
    counts,
    owners,
    own32,
    zgather,
    gather32,
    gathered,
    keys,
    futures,
    limits,
    onehot,
    scores,
    weights,
    far_send,
    far_recv,
    near_send,
    near_recv,
    zpart_send,
    zpart_recv,
    local_sem,
    archive_send,
    archive_recv,
    zg_send,
    zg_recv,
    pg_send,
    pg_recv,
    fw_send,
    fw_recv,
    ps_send,
    ps_recv,
    zs_send,
    zs_recv,
):
    wide, y = lax.axis_index("wide"), lax.axis_index("narrow")
    x, z, core = wide // 16, (wide // 2) % 8, wide % 2
    plane = x * NY + y

    def device(x, y, z, core):
        return {"wide": (x * NZ + z) * 2 + core, "narrow": y}

    def plane_peer(step):
        other_x, other_y = (x + step[0]) % NX, (y + step[1]) % NY
        return other_x * NY + other_y, device(other_x, other_y, z, core)

    twin = device(x, y, z, 1 - core)

    def remote(src, dst, send, recv, target):
        return pltpu.make_async_remote_copy(
            src_ref=src, dst_ref=dst, send_sem=send, recv_sem=recv, device_id=target, device_id_type=MESH
        )

    loads = [
        pltpu.make_async_copy(src, dst, local_sem.at[k])
        for k, (src, dst) in enumerate(
            [
                (queries_hbm, queries),
                (counts_hbm, counts),
                (owners_hbm, owners),
                (keys_hbm, keys.at[0]),
                (futures_hbm, futures.at[0]),
            ]
        )
    ]
    for load in loads:
        load.start()

    barrier = pltpu.get_barrier_semaphore()
    for step in (4, 3, 5, 2, 6, 1, 7):
        for side in range(2):
            pl.semaphore_signal(
                barrier, inc=1, device_id=device(x, y, (z + step) % NZ, side), device_id_type=MESH
            )
    for step in STEPS:
        pl.semaphore_signal(barrier, inc=1, device_id=plane_peer(step)[1], device_id_type=MESH)
    pl.semaphore_signal(barrier, inc=1, device_id=twin, device_id_type=MESH)
    loads[0].wait()
    own32[...] = queries[...].astype(jnp.float32)
    loads[1].wait()
    limits[0] = jnp.full((8, 128), counts[0], jnp.int32).astype(jnp.float32)
    pl.semaphore_wait(barrier, 2 * (NZ - 1) + PLANE - 1 + 1)

    zg_sends = []
    for step in (4, 3, 5, 2, 6, 1, 7):
        offset = (NZ - step) % NZ
        side = 0 if offset in NEAR else 1
        slot = OFFSETS[side].index(offset) * 2 + core
        copy = remote(
            own32, zgather.at[slot], zg_send.at[step], zg_recv.at[slot], device(x, y, (z + step) % NZ, side)
        )
        copy.start()
        zg_sends.append(copy)
    to_core0 = remote(own32, zgather.at[1], zg_send.at[0], zg_recv.at[1], device(x, y, z, 0))

    @pl.when(core == 1)
    def _():
        to_core0.start()

    @pl.when(core == 0)
    def _():
        zgather[0] = own32[...]

    to_twin = (
        remote(limits.at[0], limits.at[1], archive_send.at[2], archive_recv.at[2], twin),
        remote(keys_hbm, keys.at[1], archive_send.at[0], archive_recv.at[0], twin),
        remote(futures_hbm, futures.at[1], archive_send.at[1], archive_recv.at[1], twin),
    )
    for copy in to_twin:
        copy.start()

    loads[2].wait()
    position = lax.broadcasted_iota(jnp.int32, (1, MINE), 1)
    lane = lax.broadcasted_iota(jnp.int32, (32, 128), 1)
    row = lax.broadcasted_iota(jnp.int32, (32, 128), 0)
    for group in range(2):
        wanted = natural_row(0, row // 8, (z + pick((row // 2) % 4, OFFSETS[1 - group])) % NZ, core, row % 2)
        for block in range(NX):
            picked = jnp.where(lane == wanted, owners[block : block + 1, :].astype(jnp.float32), 0.0)
            owner = jnp.sum(picked, axis=1, keepdims=True)
            at = group * GROUP + block * 32
            for side in range(2):
                held = natural_row(
                    position // 64,
                    (position // 16) % 4,
                    (z + pick((position // 4) % 4, OFFSETS[side])) % NZ,
                    (position // 2) % 2,
                    position % 2,
                )
                onehot[side, at : at + 32, :] = jnp.where(
                    owner == held.astype(jnp.float32), 1.0, 0.0
                ).astype(jnp.bfloat16)

    def zg_wait(slot):
        remote(own32, zgather.at[slot], zg_send.at[0], zg_recv.at[slot], twin).wait_recv()

    for slot in range(1, 8):
        zg_wait(slot)

    @pl.when(core == 1)
    def _():
        zg_wait(0)

    for slot in range(8):
        gather32[2 * slot : 2 * slot + 2, :] = zgather[slot]
    gathered[core, plane] = gather32[...].astype(jnp.bfloat16)

    pg_sends = []
    for k, step in enumerate(STEPS):
        other, target = plane_peer(step)
        block = gathered.at[core, plane]
        copy = remote(block, block, pg_send.at[k], pg_recv.at[plane], target)
        copy.start()
        pg_sends.append(copy)

    def fw_copy(other):
        block = gathered.at[core, other]
        return remote(block, block, fw_send.at[other], fw_recv.at[other], twin)

    fw_copy(plane).start()
    for step in reversed(STEPS):
        other, target = plane_peer(step)
        block = gathered.at[core, other]
        remote(block, block, pg_send.at[0], pg_recv.at[other], target).wait_recv()
        fw_copy(other).start()

    every = gathered[core].reshape(MINE, WIDTH)
    mine = jnp.dot(onehot[core], every, preferred_element_type=jnp.float32)

    for load in loads[3:]:
        load.wait()
    for copy in to_twin:
        copy.wait()

    def fw_wait(other, carry):
        block = gathered.at[1 - core, other]
        remote(block, block, fw_send.at[other], fw_recv.at[other], twin).wait_recv()
        return carry

    lax.fori_loop(0, PLANE, fw_wait, 0)

    every = gathered[1 - core].reshape(MINE, WIDTH)
    mine = (mine + jnp.dot(onehot[1 - core], every, preferred_element_type=jnp.float32)).astype(jnp.bfloat16)

    column = lax.broadcasted_iota(jnp.int32, (1, TILE), 1).astype(jnp.float32)
    best = None
    for half in range(2):
        limit = limits[half, 0:1, 0:1]
        for tile in range(ARCHIVE // TILE):
            part = lax.dot_general(
                mine,
                keys[half, tile * TILE : (tile + 1) * TILE, :],
                (((1,), (1,)), ((), ())),
                preferred_element_type=jnp.float32,
            )
            part = jnp.where(column + float(tile * TILE) < limit, part, -1e30)
            at = half * ARCHIVE + tile * TILE
            scores[:, at : at + TILE] = part
            top = jnp.max(part, axis=1, keepdims=True)
            best = top if best is None else jnp.maximum(best, top)
    best = best.astype(jnp.bfloat16).astype(jnp.float32)
    total = jnp.zeros((MINE, 1), jnp.float32)
    for tile in range(2 * ARCHIVE // TILE):
        span = slice(tile * TILE, (tile + 1) * TILE)
        weight = jnp.exp2((scores[:, span] - best) * exponent_factor)
        weights[:, span] = weight.astype(jnp.bfloat16)
        total = total + jnp.sum(weight, axis=1, keepdims=True)

    stat_lane = lax.broadcasted_iota(jnp.int32, (1, STATS), 1)
    high = total.astype(jnp.bfloat16).astype(jnp.float32)
    stats = jnp.where(stat_lane < 32, best, jnp.where(stat_lane < 64, high, total - high))
    stats = stats.reshape(2, PLANE, 8, STATS)
    stats = jnp.stack([stats[0], stats[1]], axis=1).reshape(MINE, STATS)
    far_send[:, :, HALF:] = stats.astype(jnp.bfloat16).reshape(PLANE, ROWS, STATS)

    ps_sends = []
    for group, (send, recv) in enumerate(((far_send, far_recv), (near_send, near_recv))):
        halves = []
        for half in range(2):
            span = slice(half * HALF, (half + 1) * HALF)
            sums = None
            for side in range(2):
                term = jnp.dot(
                    weights[group * GROUP : (group + 1) * GROUP, side * ARCHIVE : (side + 1) * ARCHIVE],
                    futures[side, :, span],
                    preferred_element_type=jnp.float32,
                )
                sums = term if sums is None else sums + term
            halves.append(sums.reshape(PLANE, 8, HALF))
        sums = jnp.stack(halves, axis=1).reshape(MINE, HALF)
        send[:, :, :HALF] = sums.astype(jnp.bfloat16).reshape(PLANE, ROWS, HALF)
        for k, step in enumerate(STEPS):
            other, target = plane_peer(step)
            copy = remote(send.at[other], recv.at[plane], ps_send.at[group, k], ps_recv.at[group, plane], target)
            copy.start()
            ps_sends.append(copy)
        recv[plane] = send[plane]

    zs_sends = []
    for group, (send, recv) in enumerate(((far_send, far_recv), (near_send, near_recv))):
        for step in STEPS:
            other, target = plane_peer(step)
            remote(send.at[other], recv.at[other], ps_send.at[group, 0], ps_recv.at[group, other], target).wait_recv()
        if group == 0:
            stats = [recv[k, :, HALF:].astype(jnp.float32) for k in range(PLANE)]
            best = stats[0][:, 0:1]
            for k in range(1, PLANE):
                best = jnp.maximum(best, stats[k][:, 0:1])
            scales = [jnp.exp2((s[:, 0:1] - best) * exponent_factor) for s in stats]
            total = jnp.zeros((ROWS, 1), jnp.float32)
            for k in range(PLANE):
                total = total + (stats[k][:, 32:33] + stats[k][:, 64:65]) * scales[k]
            passed = jnp.where(stat_lane < 64, best, total)
        sums = jnp.zeros((ROWS, HALF), jnp.float32)
        for k in range(PLANE):
            scale = scales[k][group * 8 : group * 8 + 8]
            scale = jnp.concatenate([scale, scale], axis=0)
            sums = sums + recv[k, :, :HALF].astype(jnp.float32) * scale
        for index, offset in enumerate(OFFSETS[1 - group]):
            slot = group * 4 + index
            zpart_send[slot, :, :HALF] = sums[2 * index : 2 * index + 2, :]
            zpart_send[slot, :, HALF:WIDTH] = sums[8 + 2 * index : 8 + 2 * index + 2, :]
            zpart_send[slot, :, WIDTH:] = passed[group * 8 + 2 * index : group * 8 + 2 * index + 2, :]
        for index, offset in enumerate(OFFSETS[1 - group]):
            slot = group * 4 + index
            if offset == 0:
                zpart_recv[z] = zpart_send[slot]
            else:
                copy = remote(
                    zpart_send.at[slot],
                    zpart_recv.at[z],
                    zs_send.at[offset],
                    zs_recv.at[z],
                    device(x, y, (z + offset) % NZ, core),
                )
                copy.start()
                zs_sends.append(copy)

    for step in range(1, NZ):
        other = (z + step) % NZ
        remote(zpart_send.at[0], zpart_recv.at[other], zs_send.at[0], zs_recv.at[other], twin).wait_recv()

    best = zpart_recv[0, :, WIDTH : WIDTH + 1]
    for k in range(1, NZ):
        best = jnp.maximum(best, zpart_recv[k, :, WIDTH : WIDTH + 1])
    sums = jnp.zeros((2, WIDTH), jnp.float32)
    total = jnp.zeros((2, 1), jnp.float32)
    for k in range(NZ):
        stats = zpart_recv[k, :, WIDTH:]
        scale = jnp.exp2((stats[:, 0:1] - best) * exponent_factor)
        sums = sums + zpart_recv[k, :, :WIDTH] * scale
        total = total + stats[:, 64:65] * scale
    analog = sums / total
    norm_factor = lax.rsqrt(jnp.mean(analog * analog, axis=1, keepdims=True) + 1e-06)
    out[...] = (analog * norm_factor).astype(jnp.bfloat16)

    for copy in zg_sends + pg_sends + ps_sends + zs_sends:
        copy.wait_send()

    @pl.when(core == 1)
    def _():
        to_core0.wait_send()

    def fw_sent(other, carry):
        fw_copy(other).wait_send()
        return carry

    lax.fori_loop(0, PLANE, fw_sent, 0)


def body(queries, archive_keys, futures, counts, owners):
    hbm = pl.BlockSpec(memory_space=pltpu.HBM)
    dma = pltpu.SemaphoreType.DMA
    bf16, f32 = jnp.bfloat16, jnp.float32
    return pl.pallas_call(
        kernel,
        out_shape=jax.ShapeDtypeStruct((2, WIDTH), bf16),
        in_specs=[hbm] * 5,
        out_specs=pl.BlockSpec(memory_space=pltpu.VMEM),
        scratch_shapes=[
            pltpu.VMEM((2, WIDTH), bf16),
            pltpu.SMEM((1,), jnp.int32),
            pltpu.VMEM((4, 128), jnp.int32),
            pltpu.VMEM((2, WIDTH), f32),
            pltpu.VMEM((8, 2, WIDTH), f32),
            pltpu.VMEM((ROWS, WIDTH), f32),
            pltpu.VMEM((2, PLANE, ROWS, WIDTH), bf16),
            pltpu.VMEM((2, ARCHIVE, WIDTH), bf16),
            pltpu.VMEM((2, ARCHIVE, WIDTH), bf16),
            pltpu.VMEM((2, 8, 128), f32),
            pltpu.VMEM((2, MINE, MINE), bf16),
            pltpu.VMEM((MINE, 2 * ARCHIVE), f32),
            pltpu.VMEM((MINE, 2 * ARCHIVE), bf16),
            pltpu.VMEM((PLANE, ROWS, HALF + STATS), bf16),
            pltpu.VMEM((PLANE, ROWS, HALF + STATS), bf16),
            pltpu.VMEM((PLANE, ROWS, HALF), bf16),
            pltpu.VMEM((PLANE, ROWS, HALF), bf16),
            pltpu.VMEM((NZ, 2, WIDTH + STATS), f32),
            pltpu.VMEM((NZ, 2, WIDTH + STATS), f32),
            dma((5,)),
            dma((3,)),
            dma((3,)),
            dma((NZ,)),
            dma((NZ,)),
            dma((PLANE,)),
            dma((PLANE,)),
            dma((PLANE,)),
            dma((PLANE,)),
            dma((2, PLANE)),
            dma((2, PLANE)),
            dma((NZ,)),
            dma((NZ,)),
        ],
        compiler_params=pltpu.CompilerParams(
            collective_id=0, has_side_effects=True, vmem_limit_bytes=60 * 2**20
        ),
        name="analog_forecast",
    )(queries, archive_keys, futures, counts, owners.reshape(4, 128))


def solution(mesh):
    rows = P(("wide", "narrow"), None)
    return jax.shard_map(
        body,
        mesh=mesh,
        in_specs=(rows, rows, rows, P(("wide", "narrow")), P()),
        out_specs=rows,
        check_vma=False,
    )
```

```python
import jax
import jax.numpy as jnp
from jax import lax
from jax.experimental import pallas as pl
from jax.experimental.pallas import tpu as pltpu
from jax.sharding import PartitionSpec as P

MESH = pl.DeviceIdType.MESH

NX, NY, NZ = 4, 4, 8
PLANE = NX * NY
ROWS = 16
MINE = PLANE * ROWS
GROUP = MINE // 2
WIDTH = 1024
HALF = 512
STATS = 128
ARCHIVE = 768
TILE = 256

NEAR, FAR = (0, 1, 7, 6), (4, 3, 5, 2)
OFFSETS = NEAR, FAR

STEPS = sorted(
    [(a, b) for a in range(NX) for b in range(NY) if a or b],
    key=lambda s: -(min(s[0], NX - s[0]) + min(s[1], NY - s[1])),
)

score_scale = 3.0
exponent_factor = score_scale / 32.0 * 1.4426950408889634


def pick(index, values):
    result = jnp.full_like(index, values[0])
    for k in range(1, len(values)):
        result = jnp.where(index == k, values[k], result)
    return result


def natural_row(x, y, z, core, row):
    return x * 128 + z * 16 + core * 8 + y * 2 + row


def kernel(
    queries_hbm,
    keys_hbm,
    futures_hbm,
    counts_hbm,
    owners_hbm,
    out,
    queries,
    counts,
    owners,
    own32,
    zgather,
    gather32,
    gathered,
    keys,
    futures,
    limits,
    onehot,
    scores,
    weights,
    far_send,
    far_recv,
    near_send,
    near_recv,
    zpart_send,
    zpart_recv,
    local_sem,
    archive_send,
    archive_recv,
    zg_send,
    zg_recv,
    pg_send,
    pg_recv,
    fw_send,
    fw_recv,
    ps_send,
    ps_recv,
    zs_send,
    zs_recv,
):
    wide, y = lax.axis_index("wide"), lax.axis_index("narrow")
    x, z, core = wide // 16, (wide // 2) % 8, wide % 2
    plane = x * NY + y

    def device(x, y, z, core):
        return {"wide": (x * NZ + z) * 2 + core, "narrow": y}

    def plane_peer(step):
        other_x, other_y = (x + step[0]) % NX, (y + step[1]) % NY
        return other_x * NY + other_y, device(other_x, other_y, z, core)

    twin = device(x, y, z, 1 - core)

    def remote(src, dst, send, recv, target):
        return pltpu.make_async_remote_copy(
            src_ref=src, dst_ref=dst, send_sem=send, recv_sem=recv, device_id=target, device_id_type=MESH
        )

    loads = [
        pltpu.make_async_copy(src, dst, local_sem.at[k])
        for k, (src, dst) in enumerate(
            [
                (queries_hbm, queries),
                (counts_hbm, counts),
                (owners_hbm, owners),
                (keys_hbm, keys.at[0]),
                (futures_hbm, futures.at[0]),
            ]
        )
    ]
    for load in loads:
        load.start()

    barrier = pltpu.get_barrier_semaphore()
    for step in (4, 3, 5, 2, 6, 1, 7):
        for side in range(2):
            pl.semaphore_signal(
                barrier, inc=1, device_id=device(x, y, (z + step) % NZ, side), device_id_type=MESH
            )
    for step in STEPS:
        pl.semaphore_signal(barrier, inc=1, device_id=plane_peer(step)[1], device_id_type=MESH)
    pl.semaphore_signal(barrier, inc=1, device_id=twin, device_id_type=MESH)
    loads[0].wait()
    own32[...] = queries[...].astype(jnp.float32)
    loads[1].wait()
    limits[0] = jnp.full((8, 128), counts[0], jnp.int32).astype(jnp.float32)
    pl.semaphore_wait(barrier, 2 * (NZ - 1) + PLANE - 1 + 1)

    zg_sends = []
    for step in (4, 3, 5, 2, 6, 1, 7):
        offset = (NZ - step) % NZ
        side = 0 if offset in NEAR else 1
        slot = OFFSETS[side].index(offset) * 2 + core
        copy = remote(
            own32, zgather.at[slot], zg_send.at[step], zg_recv.at[slot], device(x, y, (z + step) % NZ, side)
        )
        copy.start()
        zg_sends.append(copy)
    to_core0 = remote(own32, zgather.at[1], zg_send.at[0], zg_recv.at[1], device(x, y, z, 0))

    @pl.when(core == 1)
    def _():
        to_core0.start()

    @pl.when(core == 0)
    def _():
        zgather[0] = own32[...]

    to_twin = (
        remote(limits.at[0], limits.at[1], archive_send.at[2], archive_recv.at[2], twin),
        remote(keys_hbm, keys.at[1], archive_send.at[0], archive_recv.at[0], twin),
        remote(futures_hbm, futures.at[1], archive_send.at[1], archive_recv.at[1], twin),
    )
    for copy in to_twin:
        copy.start()

    loads[2].wait()
    position = lax.broadcasted_iota(jnp.int32, (1, MINE), 1)
    lane = lax.broadcasted_iota(jnp.int32, (32, 128), 1)
    row = lax.broadcasted_iota(jnp.int32, (32, 128), 0)
    for group in range(2):
        wanted = natural_row(0, row // 8, (z + pick((row // 2) % 4, OFFSETS[1 - group])) % NZ, core, row % 2)
        for block in range(NX):
            picked = jnp.where(lane == wanted, owners[block : block + 1, :].astype(jnp.float32), 0.0)
            owner = jnp.sum(picked, axis=1, keepdims=True)
            at = group * GROUP + block * 32
            for side in range(2):
                held = natural_row(
                    position // 64,
                    (position // 16) % 4,
                    (z + pick((position // 4) % 4, OFFSETS[side])) % NZ,
                    (position // 2) % 2,
                    position % 2,
                )
                onehot[side, at : at + 32, :] = jnp.where(
                    owner == held.astype(jnp.float32), 1.0, 0.0
                ).astype(jnp.bfloat16)

    def zg_wait(slot):
        remote(own32, zgather.at[slot], zg_send.at[0], zg_recv.at[slot], twin).wait_recv()

    for slot in range(1, 8):
        zg_wait(slot)

    @pl.when(core == 1)
    def _():
        zg_wait(0)

    for slot in range(8):
        gather32[2 * slot : 2 * slot + 2, :] = zgather[slot]
    gathered[core, plane] = gather32[...].astype(jnp.bfloat16)

    pg_sends = []
    for k, step in enumerate(STEPS):
        other, target = plane_peer(step)
        block = gathered.at[core, plane]
        copy = remote(block, block, pg_send.at[k], pg_recv.at[plane], target)
        copy.start()
        pg_sends.append(copy)

    def fw_copy(other):
        block = gathered.at[core, other]
        return remote(block, block, fw_send.at[other], fw_recv.at[other], twin)

    fw_copy(plane).start()
    for step in reversed(STEPS):
        other, target = plane_peer(step)
        block = gathered.at[core, other]
        remote(block, block, pg_send.at[0], pg_recv.at[other], target).wait_recv()
        fw_copy(other).start()

    every = gathered[core].reshape(MINE, WIDTH)
    mine = jnp.dot(onehot[core], every, preferred_element_type=jnp.float32)

    for load in loads[3:]:
        load.wait()
    for copy in to_twin:
        copy.wait()

    def fw_wait(other, carry):
        block = gathered.at[1 - core, other]
        remote(block, block, fw_send.at[other], fw_recv.at[other], twin).wait_recv()
        return carry

    lax.fori_loop(0, PLANE, fw_wait, 0)

    every = gathered[1 - core].reshape(MINE, WIDTH)
    mine = (mine + jnp.dot(onehot[1 - core], every, preferred_element_type=jnp.float32)).astype(jnp.bfloat16)

    column = lax.broadcasted_iota(jnp.int32, (1, TILE), 1).astype(jnp.float32)
    best = None
    for half in range(2):
        limit = limits[half, 0:1, 0:1]
        for tile in range(ARCHIVE // TILE):
            part = lax.dot_general(
                mine,
                keys[half, tile * TILE : (tile + 1) * TILE, :],
                (((1,), (1,)), ((), ())),
                preferred_element_type=jnp.float32,
            )
            part = jnp.where(column + float(tile * TILE) < limit, part, -1e30)
            at = half * ARCHIVE + tile * TILE
            scores[:, at : at + TILE] = part
            top = jnp.max(part, axis=1, keepdims=True)
            best = top if best is None else jnp.maximum(best, top)
    best = best.astype(jnp.bfloat16).astype(jnp.float32)
    total = jnp.zeros((MINE, 1), jnp.float32)
    for tile in range(2 * ARCHIVE // TILE):
        span = slice(tile * TILE, (tile + 1) * TILE)
        weight = jnp.exp2((scores[:, span] - best) * exponent_factor)
        weights[:, span] = weight.astype(jnp.bfloat16)
        total = total + jnp.sum(weight, axis=1, keepdims=True)

    stat_lane = lax.broadcasted_iota(jnp.int32, (1, STATS), 1)
    high = total.astype(jnp.bfloat16).astype(jnp.float32)
    stats = jnp.where(stat_lane < 32, best, jnp.where(stat_lane < 64, high, total - high))
    stats = stats.reshape(2, PLANE, 8, STATS)
    stats = jnp.stack([stats[0], stats[1]], axis=1).reshape(MINE, STATS)
    far_send[:, :, HALF:] = stats.astype(jnp.bfloat16).reshape(PLANE, ROWS, STATS)

    ps_sends = []
    for group, (send, recv) in enumerate(((far_send, far_recv), (near_send, near_recv))):
        halves = []
        for half in range(2):
            span = slice(half * HALF, (half + 1) * HALF)
            sums = None
            for side in range(2):
                term = jnp.dot(
                    weights[group * GROUP : (group + 1) * GROUP, side * ARCHIVE : (side + 1) * ARCHIVE],
                    futures[side, :, span],
                    preferred_element_type=jnp.float32,
                )
                sums = term if sums is None else sums + term
            halves.append(sums.reshape(PLANE, 8, HALF))
        sums = jnp.stack(halves, axis=1).reshape(MINE, HALF)
        send[:, :, :HALF] = sums.astype(jnp.bfloat16).reshape(PLANE, ROWS, HALF)
        for k, step in enumerate(STEPS):
            other, target = plane_peer(step)
            copy = remote(send.at[other], recv.at[plane], ps_send.at[group, k], ps_recv.at[group, plane], target)
            copy.start()
            ps_sends.append(copy)
        recv[plane] = send[plane]

    zs_sends = []
    for group, (send, recv) in enumerate(((far_send, far_recv), (near_send, near_recv))):
        for step in STEPS:
            other, target = plane_peer(step)
            remote(send.at[other], recv.at[other], ps_send.at[group, 0], ps_recv.at[group, other], target).wait_recv()
        if group == 0:
            stats = [recv[k, :, HALF:].astype(jnp.float32) for k in range(PLANE)]
            best = stats[0][:, 0:1]
            for k in range(1, PLANE):
                best = jnp.maximum(best, stats[k][:, 0:1])
            scales = [jnp.exp2((s[:, 0:1] - best) * exponent_factor) for s in stats]
            total = jnp.zeros((ROWS, 1), jnp.float32)
            for k in range(PLANE):
                total = total + (stats[k][:, 32:33] + stats[k][:, 64:65]) * scales[k]
            passed = jnp.where(stat_lane < 64, best, total)
        sums = jnp.zeros((ROWS, HALF), jnp.float32)
        for k in range(PLANE):
            scale = scales[k][group * 8 : group * 8 + 8]
            scale = jnp.concatenate([scale, scale], axis=0)
            sums = sums + recv[k, :, :HALF].astype(jnp.float32) * scale
        for index, offset in enumerate(OFFSETS[1 - group]):
            slot = group * 4 + index
            zpart_send[slot, :, :HALF] = sums[2 * index : 2 * index + 2, :]
            zpart_send[slot, :, HALF:WIDTH] = sums[8 + 2 * index : 8 + 2 * index + 2, :]
            zpart_send[slot, :, WIDTH:] = passed[group * 8 + 2 * index : group * 8 + 2 * index + 2, :]
        for index, offset in enumerate(OFFSETS[1 - group]):
            slot = group * 4 + index
            if offset == 0:
                zpart_recv[z] = zpart_send[slot]
            else:
                copy = remote(
                    zpart_send.at[slot],
                    zpart_recv.at[z],
                    zs_send.at[offset],
                    zs_recv.at[z],
                    device(x, y, (z + offset) % NZ, core),
                )
                copy.start()
                zs_sends.append(copy)

    for step in range(1, NZ):
        other = (z + step) % NZ
        remote(zpart_send.at[0], zpart_recv.at[other], zs_send.at[0], zs_recv.at[other], twin).wait_recv()

    best = zpart_recv[0, :, WIDTH : WIDTH + 1]
    for k in range(1, NZ):
        best = jnp.maximum(best, zpart_recv[k, :, WIDTH : WIDTH + 1])
    sums = jnp.zeros((2, WIDTH), jnp.float32)
    total = jnp.zeros((2, 1), jnp.float32)
    for k in range(NZ):
        stats = zpart_recv[k, :, WIDTH:]
        scale = jnp.exp2((stats[:, 0:1] - best) * exponent_factor)
        sums = sums + zpart_recv[k, :, :WIDTH] * scale
        total = total + stats[:, 64:65] * scale
    analog = sums / total
    norm_factor = lax.rsqrt(jnp.mean(analog * analog, axis=1, keepdims=True) + 1e-06)
    out[...] = (analog * norm_factor).astype(jnp.bfloat16)

    for copy in zg_sends + pg_sends + ps_sends + zs_sends:
        copy.wait_send()

    @pl.when(core == 1)
    def _():
        to_core0.wait_send()

    def fw_sent(other, carry):
        fw_copy(other).wait_send()
        return carry

    lax.fori_loop(0, PLANE, fw_sent, 0)


def in_hbm(array):
    return pltpu.with_memory_space_constraint(array, pltpu.HBM)


def body(queries, archive_keys, futures, counts, owners):
    hbm = pl.BlockSpec(memory_space=pltpu.HBM)
    dma = pltpu.SemaphoreType.DMA
    bf16, f32 = jnp.bfloat16, jnp.float32
    return pl.pallas_call(
        kernel,
        out_shape=jax.ShapeDtypeStruct((2, WIDTH), bf16),
        in_specs=[hbm] * 5,
        out_specs=pl.BlockSpec(memory_space=pltpu.VMEM),
        scratch_shapes=[
            pltpu.VMEM((2, WIDTH), bf16),
            pltpu.SMEM((1,), jnp.int32),
            pltpu.VMEM((4, 128), jnp.int32),
            pltpu.VMEM((2, WIDTH), f32),
            pltpu.VMEM((8, 2, WIDTH), f32),
            pltpu.VMEM((ROWS, WIDTH), f32),
            pltpu.VMEM((2, PLANE, ROWS, WIDTH), bf16),
            pltpu.VMEM((2, ARCHIVE, WIDTH), bf16),
            pltpu.VMEM((2, ARCHIVE, WIDTH), bf16),
            pltpu.VMEM((2, 8, 128), f32),
            pltpu.VMEM((2, MINE, MINE), bf16),
            pltpu.VMEM((MINE, 2 * ARCHIVE), f32),
            pltpu.VMEM((MINE, 2 * ARCHIVE), bf16),
            pltpu.VMEM((PLANE, ROWS, HALF + STATS), bf16),
            pltpu.VMEM((PLANE, ROWS, HALF + STATS), bf16),
            pltpu.VMEM((PLANE, ROWS, HALF), bf16),
            pltpu.VMEM((PLANE, ROWS, HALF), bf16),
            pltpu.VMEM((NZ, 2, WIDTH + STATS), f32),
            pltpu.VMEM((NZ, 2, WIDTH + STATS), f32),
            dma((5,)),
            dma((3,)),
            dma((3,)),
            dma((NZ,)),
            dma((NZ,)),
            dma((PLANE,)),
            dma((PLANE,)),
            dma((PLANE,)),
            dma((PLANE,)),
            dma((2, PLANE)),
            dma((2, PLANE)),
            dma((NZ,)),
            dma((NZ,)),
        ],
        compiler_params=pltpu.CompilerParams(
            collective_id=0, has_side_effects=True, vmem_limit_bytes=40 * 2**20
        ),
        name="analog_forecast",
    )(in_hbm(queries), in_hbm(archive_keys), in_hbm(futures), counts, in_hbm(owners.reshape(4, 128)))


def solution(mesh):
    rows = P(("wide", "narrow"), None)
    return jax.shard_map(
        body,
        mesh=mesh,
        in_specs=(rows, rows, rows, P(("wide", "narrow")), P()),
        out_specs=rows,
        check_vma=False,
    )
```

```python
import jax
import jax.numpy as jnp
from jax import lax
from jax.experimental import pallas as pl
from jax.experimental.pallas import tpu as pltpu
from jax.sharding import PartitionSpec as P

MESH = pl.DeviceIdType.MESH

NX, NY, NZ = 4, 4, 8
PLANE = NX * NY
ROWS = 16
MINE = PLANE * ROWS
GROUP = MINE // 2
WIDTH = 1024
HALF = 512
STATS = 128
ARCHIVE = 768
TILE = 256

NEAR, FAR = (0, 1, 7, 6), (4, 3, 5, 2)
OFFSETS = NEAR, FAR

STEPS = sorted(
    [(a, b) for a in range(NX) for b in range(NY) if a or b],
    key=lambda s: -(min(s[0], NX - s[0]) + min(s[1], NY - s[1])),
)

score_scale = 3.0
exponent_factor = score_scale / 32.0 * 1.4426950408889634


def pick(index, values):
    result = jnp.full_like(index, values[0])
    for k in range(1, len(values)):
        result = jnp.where(index == k, values[k], result)
    return result


def natural_row(x, y, z, core, row):
    return x * 128 + z * 16 + core * 8 + y * 2 + row


def kernel(
    queries_hbm,
    keys_hbm,
    futures_hbm,
    counts_hbm,
    owners_hbm,
    out,
    queries,
    counts,
    owners,
    own32,
    zgather,
    gather32,
    gathered,
    keys,
    futures,
    limits,
    onehot,
    scores,
    weights,
    far_send,
    far_recv,
    near_send,
    near_recv,
    stat_send,
    stat_recv,
    zpart_send,
    zpart_recv,
    local_sem,
    archive_send,
    archive_recv,
    zg_send,
    zg_recv,
    pg_send,
    pg_recv,
    fw_send,
    fw_recv,
    ps_send,
    ps_recv,
    st_send,
    st_recv,
    zs_send,
    zs_recv,
):
    wide, y = lax.axis_index("wide"), lax.axis_index("narrow")
    x, z, core = wide // 16, (wide // 2) % 8, wide % 2
    plane = x * NY + y

    def device(x, y, z, core):
        return {"wide": (x * NZ + z) * 2 + core, "narrow": y}

    def plane_peer(step):
        other_x, other_y = (x + step[0]) % NX, (y + step[1]) % NY
        return other_x * NY + other_y, device(other_x, other_y, z, core)

    twin = device(x, y, z, 1 - core)

    def remote(src, dst, send, recv, target):
        return pltpu.make_async_remote_copy(
            src_ref=src, dst_ref=dst, send_sem=send, recv_sem=recv, device_id=target, device_id_type=MESH
        )

    loads = [
        pltpu.make_async_copy(src, dst, local_sem.at[k])
        for k, (src, dst) in enumerate(
            [
                (queries_hbm, queries),
                (counts_hbm, counts),
                (owners_hbm, owners),
                (keys_hbm, keys.at[0]),
                (futures_hbm, futures.at[0]),
            ]
        )
    ]
    loads[0].start()
    loads[1].start()

    barrier = pltpu.get_barrier_semaphore()
    for step in (4, 3, 5, 2, 6, 1, 7):
        for side in range(2):
            pl.semaphore_signal(
                barrier, inc=1, device_id=device(x, y, (z + step) % NZ, side), device_id_type=MESH
            )
    for step in STEPS:
        pl.semaphore_signal(barrier, inc=1, device_id=plane_peer(step)[1], device_id_type=MESH)
    pl.semaphore_signal(barrier, inc=1, device_id=twin, device_id_type=MESH)
    for load in loads[2:]:
        load.start()
    loads[0].wait()
    own32[...] = queries[...].astype(jnp.float32)
    loads[1].wait()
    limits[0] = jnp.full((8, 128), counts[0], jnp.int32).astype(jnp.float32)
    pl.semaphore_wait(barrier, 2 * (NZ - 1) + PLANE - 1 + 1)

    zg_sends = []
    for step in (4, 3, 5, 2, 6, 1, 7):
        offset = (NZ - step) % NZ
        side = 0 if offset in NEAR else 1
        slot = OFFSETS[side].index(offset) * 2 + core
        copy = remote(
            own32, zgather.at[slot], zg_send.at[step], zg_recv.at[slot], device(x, y, (z + step) % NZ, side)
        )
        copy.start()
        zg_sends.append(copy)
    to_core0 = remote(own32, zgather.at[1], zg_send.at[0], zg_recv.at[1], device(x, y, z, 0))

    @pl.when(core == 1)
    def _():
        to_core0.start()

    @pl.when(core == 0)
    def _():
        zgather[0] = own32[...]

    to_twin = (
        remote(limits.at[0], limits.at[1], archive_send.at[2], archive_recv.at[2], twin),
        remote(keys_hbm, keys.at[1], archive_send.at[0], archive_recv.at[0], twin),
        remote(futures_hbm, futures.at[1], archive_send.at[1], archive_recv.at[1], twin),
    )
    for copy in to_twin:
        copy.start()

    loads[2].wait()
    position = lax.broadcasted_iota(jnp.int32, (1, MINE), 1)
    lane = lax.broadcasted_iota(jnp.int32, (32, 128), 1)
    row = lax.broadcasted_iota(jnp.int32, (32, 128), 0)
    for group in range(2):
        wanted = natural_row(0, row // 8, (z + pick((row // 2) % 4, OFFSETS[1 - group])) % NZ, core, row % 2)
        for block in range(NX):
            picked = jnp.where(lane == wanted, owners[block : block + 1, :].astype(jnp.float32), 0.0)
            owner = jnp.sum(picked, axis=1, keepdims=True)
            at = group * GROUP + block * 32
            for side in range(2):
                held = natural_row(
                    position // 64,
                    (position // 16) % 4,
                    (z + pick((position // 4) % 4, OFFSETS[side])) % NZ,
                    (position // 2) % 2,
                    position % 2,
                )
                onehot[side, at : at + 32, :] = jnp.where(
                    owner == held.astype(jnp.float32), 1.0, 0.0
                ).astype(jnp.bfloat16)

    def zg_wait(slot):
        remote(own32, zgather.at[slot], zg_send.at[0], zg_recv.at[slot], twin).wait_recv()

    for slot in range(1, 8):
        zg_wait(slot)

    @pl.when(core == 1)
    def _():
        zg_wait(0)

    for slot in range(8):
        gather32[2 * slot : 2 * slot + 2, :] = zgather[slot]
    gathered[core, plane] = gather32[...].astype(jnp.bfloat16)

    pg_sends = []
    for k, step in enumerate(STEPS):
        other, target = plane_peer(step)
        block = gathered.at[core, plane]
        copy = remote(block, block, pg_send.at[k], pg_recv.at[plane], target)
        copy.start()
        pg_sends.append(copy)

    def fw_copy(other):
        block = gathered.at[core, other]
        return remote(block, block, fw_send.at[other], fw_recv.at[other], twin)

    fw_copy(plane).start()
    for step in STEPS:
        other, target = plane_peer(step)
        block = gathered.at[core, other]
        remote(block, block, pg_send.at[0], pg_recv.at[other], target).wait_recv()
        fw_copy(other).start()

    every = gathered[core].reshape(MINE, WIDTH)
    mine = jnp.dot(onehot[core], every, preferred_element_type=jnp.float32)

    for load in loads[3:]:
        load.wait()
    for copy in to_twin:
        copy.wait()

    def fw_wait(other, carry):
        block = gathered.at[1 - core, other]
        remote(block, block, fw_send.at[other], fw_recv.at[other], twin).wait_recv()
        return carry

    lax.fori_loop(0, PLANE, fw_wait, 0)

    every = gathered[1 - core].reshape(MINE, WIDTH)
    mine = (mine + jnp.dot(onehot[1 - core], every, preferred_element_type=jnp.float32)).astype(jnp.bfloat16)

    column = lax.broadcasted_iota(jnp.int32, (1, TILE), 1).astype(jnp.float32)
    best = None
    for half in range(2):
        limit = limits[half, 0:1, 0:1]
        for tile in range(ARCHIVE // TILE):
            part = lax.dot_general(
                mine,
                keys[half, tile * TILE : (tile + 1) * TILE, :],
                (((1,), (1,)), ((), ())),
                preferred_element_type=jnp.float32,
            )
            if tile > 0:
                part = jnp.where(column + float(tile * TILE) < limit, part, -1e30)
            at = half * ARCHIVE + tile * TILE
            scores[:, at : at + TILE] = part
            top = jnp.max(part, axis=1, keepdims=True)
            best = top if best is None else jnp.maximum(best, top)
    total = jnp.zeros((MINE, 1), jnp.float32)
    for tile in range(2 * ARCHIVE // TILE):
        span = slice(tile * TILE, (tile + 1) * TILE)
        weight = jnp.exp2((scores[:, span] - best) * exponent_factor)
        weights[:, span] = weight.astype(jnp.bfloat16)
        total = total + jnp.sum(weight, axis=1, keepdims=True)

    stat_lane = lax.broadcasted_iota(jnp.int32, (MINE, STATS), 1)
    stat_row = lax.broadcasted_iota(jnp.int32, (MINE, STATS), 0)
    stat_here = stat_lane == (stat_row // GROUP) * 8 + stat_row % 8
    for k, value in enumerate((best, total)):
        value = jnp.where(stat_here, value, 0.0).reshape(2, PLANE, 8, STATS)
        stat_send[:, k : k + 1, :] = jnp.sum(value[0] + value[1], axis=1, keepdims=True)
    st_sends = []
    for k, step in enumerate(STEPS):
        other, target = plane_peer(step)
        copy = remote(stat_send.at[other], stat_recv.at[plane], st_send.at[k], st_recv.at[plane], target)
        copy.start()
        st_sends.append(copy)
    stat_recv[plane] = stat_send[plane]

    ps_sends = []
    for group, (send, recv) in enumerate(((far_send, far_recv), (near_send, near_recv))):
        halves = []
        for half in range(2):
            span = slice(half * HALF, (half + 1) * HALF)
            sums = None
            for side in range(2):
                term = jnp.dot(
                    weights[group * GROUP : (group + 1) * GROUP, side * ARCHIVE : (side + 1) * ARCHIVE],
                    futures[side, :, span],
                    preferred_element_type=jnp.float32,
                )
                sums = term if sums is None else sums + term
            halves.append(sums.reshape(PLANE, 8, HALF))
        sums = jnp.stack(halves, axis=1).reshape(MINE, HALF)
        send[...] = sums.astype(jnp.bfloat16).reshape(PLANE, ROWS, HALF)
        for k, step in enumerate(STEPS):
            other, target = plane_peer(step)
            copy = remote(send.at[other], recv.at[plane], ps_send.at[group, k], ps_recv.at[group, plane], target)
            copy.start()
            ps_sends.append(copy)
        recv[plane] = send[plane]

    for step in STEPS:
        other, target = plane_peer(step)
        remote(stat_send.at[other], stat_recv.at[other], st_send.at[0], st_recv.at[other], target).wait_recv()
    at_row = lax.broadcasted_iota(jnp.int32, (ROWS, STATS), 0) == lax.broadcasted_iota(jnp.int32, (ROWS, STATS), 1)

    def upright(value):
        return jnp.sum(jnp.where(at_row, value, 0.0), axis=1, keepdims=True)

    maxima = [stat_recv[k, 0:1, :] for k in range(PLANE)]
    best = maxima[0]
    for k in range(1, PLANE):
        best = jnp.maximum(best, maxima[k])
    scales = [jnp.exp2((m - best) * exponent_factor) for m in maxima]
    total = jnp.zeros((1, STATS), jnp.float32)
    for k in range(PLANE):
        total = total + stat_recv[k, 1:2, :] * scales[k]
    scales = [upright(scale) for scale in scales]
    passed_lane = lax.broadcasted_iota(jnp.int32, (1, STATS), 1)
    passed = jnp.where(passed_lane < 64, upright(best), upright(total))

    zs_sends = []
    for group, (send, recv) in enumerate(((far_send, far_recv), (near_send, near_recv))):
        for step in STEPS:
            other, target = plane_peer(step)
            remote(send.at[other], recv.at[other], ps_send.at[group, 0], ps_recv.at[group, other], target).wait_recv()
        sums = jnp.zeros((ROWS, HALF), jnp.float32)
        for k in range(PLANE):
            scale = scales[k][group * 8 : group * 8 + 8]
            scale = jnp.concatenate([scale, scale], axis=0)
            sums = sums + recv[k].astype(jnp.float32) * scale
        for index, offset in enumerate(OFFSETS[1 - group]):
            slot = group * 4 + index
            zpart_send[slot, :, :HALF] = sums[2 * index : 2 * index + 2, :]
            zpart_send[slot, :, HALF:WIDTH] = sums[8 + 2 * index : 8 + 2 * index + 2, :]
            zpart_send[slot, :, WIDTH:] = passed[group * 8 + 2 * index : group * 8 + 2 * index + 2, :]
        for index, offset in enumerate(OFFSETS[1 - group]):
            slot = group * 4 + index
            if offset == 0:
                zpart_recv[z] = zpart_send[slot]
            else:
                copy = remote(
                    zpart_send.at[slot],
                    zpart_recv.at[z],
                    zs_send.at[offset],
                    zs_recv.at[z],
                    device(x, y, (z + offset) % NZ, core),
                )
                copy.start()
                zs_sends.append(copy)

    for step in range(1, NZ):
        other = (z + step) % NZ
        remote(zpart_send.at[0], zpart_recv.at[other], zs_send.at[0], zs_recv.at[other], twin).wait_recv()

    best = zpart_recv[0, :, WIDTH : WIDTH + 1]
    for k in range(1, NZ):
        best = jnp.maximum(best, zpart_recv[k, :, WIDTH : WIDTH + 1])
    sums = jnp.zeros((2, WIDTH), jnp.float32)
    total = jnp.zeros((2, 1), jnp.float32)
    for k in range(NZ):
        stats = zpart_recv[k, :, WIDTH:]
        scale = jnp.exp2((stats[:, 0:1] - best) * exponent_factor)
        sums = sums + zpart_recv[k, :, :WIDTH] * scale
        total = total + stats[:, 64:65] * scale
    analog = sums / total
    norm_factor = lax.rsqrt(jnp.mean(analog * analog, axis=1, keepdims=True) + 1e-06)
    out[...] = (analog * norm_factor).astype(jnp.bfloat16)

    for copy in zg_sends + pg_sends + st_sends + ps_sends + zs_sends:
        copy.wait_send()

    @pl.when(core == 1)
    def _():
        to_core0.wait_send()

    def fw_sent(other, carry):
        fw_copy(other).wait_send()
        return carry

    lax.fori_loop(0, PLANE, fw_sent, 0)


def in_hbm(array):
    return pltpu.with_memory_space_constraint(array, pltpu.HBM)


def body(queries, archive_keys, futures, counts, owners):
    hbm = pl.BlockSpec(memory_space=pltpu.HBM)
    dma = pltpu.SemaphoreType.DMA
    bf16, f32 = jnp.bfloat16, jnp.float32
    return pl.pallas_call(
        kernel,
        out_shape=jax.ShapeDtypeStruct((2, WIDTH), bf16),
        in_specs=[hbm] * 5,
        out_specs=pl.BlockSpec(memory_space=pltpu.VMEM),
        scratch_shapes=[
            pltpu.VMEM((2, WIDTH), bf16),
            pltpu.SMEM((1,), jnp.int32),
            pltpu.VMEM((4, 128), jnp.int32),
            pltpu.VMEM((2, WIDTH), f32),
            pltpu.VMEM((8, 2, WIDTH), f32),
            pltpu.VMEM((ROWS, WIDTH), f32),
            pltpu.VMEM((2, PLANE, ROWS, WIDTH), bf16),
            pltpu.VMEM((2, ARCHIVE, WIDTH), bf16),
            pltpu.VMEM((2, ARCHIVE, WIDTH), bf16),
            pltpu.VMEM((2, 8, 128), f32),
            pltpu.VMEM((2, MINE, MINE), bf16),
            pltpu.VMEM((MINE, 2 * ARCHIVE), f32),
            pltpu.VMEM((MINE, 2 * ARCHIVE), bf16),
            pltpu.VMEM((PLANE, ROWS, HALF), bf16),
            pltpu.VMEM((PLANE, ROWS, HALF), bf16),
            pltpu.VMEM((PLANE, ROWS, HALF), bf16),
            pltpu.VMEM((PLANE, ROWS, HALF), bf16),
            pltpu.VMEM((PLANE, 2, STATS), f32),
            pltpu.VMEM((PLANE, 2, STATS), f32),
            pltpu.VMEM((NZ, 2, WIDTH + STATS), f32),
            pltpu.VMEM((NZ, 2, WIDTH + STATS), f32),
            dma((5,)),
            dma((3,)),
            dma((3,)),
            dma((NZ,)),
            dma((NZ,)),
            dma((PLANE,)),
            dma((PLANE,)),
            dma((PLANE,)),
            dma((PLANE,)),
            dma((2, PLANE)),
            dma((2, PLANE)),
            dma((PLANE,)),
            dma((PLANE,)),
            dma((NZ,)),
            dma((NZ,)),
        ],
        compiler_params=pltpu.CompilerParams(
            collective_id=0, has_side_effects=True, vmem_limit_bytes=40 * 2**20
        ),
        name="analog_forecast",
    )(in_hbm(queries), in_hbm(archive_keys), in_hbm(futures), counts, in_hbm(owners.reshape(4, 128)))


def solution(mesh):
    rows = P(("wide", "narrow"), None)
    return jax.shard_map(
        body,
        mesh=mesh,
        in_specs=(rows, rows, rows, P(("wide", "narrow")), P()),
        out_specs=rows,
        check_vma=False,
    )
```

```python
import jax
import jax.numpy as jnp
from jax import lax
from jax.experimental import pallas as pl
from jax.experimental.pallas import tpu as pltpu
from jax.sharding import PartitionSpec as P

MESH = pl.DeviceIdType.MESH

NX, NY, NZ = 4, 4, 8
PLANE = NX * NY
ROWS = 16
MINE = PLANE * ROWS
GROUP = MINE // 2
WIDTH = 1024
HALF = 512
STATS = 128
ARCHIVE = 768
TILE = 256

NEAR, FAR = (0, 1, 7, 6), (4, 3, 5, 2)
OFFSETS = NEAR, FAR

STEPS = sorted(
    [(a, b) for a in range(NX) for b in range(NY) if a or b],
    key=lambda s: -(min(s[0], NX - s[0]) + min(s[1], NY - s[1])),
)

score_scale = 3.0
exponent_factor = score_scale / 32.0 * 1.4426950408889634


def pick(index, values):
    result = jnp.full_like(index, values[0])
    for k in range(1, len(values)):
        result = jnp.where(index == k, values[k], result)
    return result


def natural_row(x, y, z, core, row):
    return x * 128 + z * 16 + core * 8 + y * 2 + row


def kernel(
    queries_hbm,
    keys_hbm,
    futures_hbm,
    counts_hbm,
    owners_hbm,
    out,
    queries,
    counts,
    owners,
    own32,
    zgather,
    gather32,
    gathered,
    keys,
    futures,
    limits,
    onehot,
    scores,
    weights,
    low_send,
    low_recv,
    high_send,
    high_recv,
    stat_send,
    stat_recv,
    zpart_send,
    zpart_recv,
    local_sem,
    archive_send,
    archive_recv,
    zg_send,
    zg_recv,
    pg_send,
    pg_recv,
    fw_send,
    fw_recv,
    ps_send,
    ps_recv,
    st_send,
    st_recv,
    zs_send,
    zs_recv,
):
    wide, y = lax.axis_index("wide"), lax.axis_index("narrow")
    x, z, core = wide // 16, (wide // 2) % 8, wide % 2
    plane = x * NY + y

    def device(x, y, z, core):
        return {"wide": (x * NZ + z) * 2 + core, "narrow": y}

    def plane_peer(step):
        other_x, other_y = (x + step[0]) % NX, (y + step[1]) % NY
        return other_x * NY + other_y, device(other_x, other_y, z, core)

    twin = device(x, y, z, 1 - core)

    def remote(src, dst, send, recv, target):
        return pltpu.make_async_remote_copy(
            src_ref=src, dst_ref=dst, send_sem=send, recv_sem=recv, device_id=target, device_id_type=MESH
        )

    loads = [
        pltpu.make_async_copy(src, dst, local_sem.at[k])
        for k, (src, dst) in enumerate(
            [
                (queries_hbm, queries),
                (counts_hbm, counts),
                (owners_hbm, owners),
                (keys_hbm, keys.at[0]),
                (futures_hbm, futures.at[0]),
            ]
        )
    ]
    loads[0].start()
    loads[1].start()

    barrier = pltpu.get_barrier_semaphore()
    for step in (4, 3, 5, 2, 6, 1, 7):
        for side in range(2):
            pl.semaphore_signal(
                barrier, inc=1, device_id=device(x, y, (z + step) % NZ, side), device_id_type=MESH
            )
    for step in STEPS:
        pl.semaphore_signal(barrier, inc=1, device_id=plane_peer(step)[1], device_id_type=MESH)
    pl.semaphore_signal(barrier, inc=1, device_id=twin, device_id_type=MESH)
    for load in loads[2:]:
        load.start()
    loads[0].wait()
    own32[...] = queries[...].astype(jnp.float32)
    loads[1].wait()
    limits[0] = jnp.full((8, 128), counts[0], jnp.int32).astype(jnp.float32)
    pl.semaphore_wait(barrier, 2 * (NZ - 1) + PLANE - 1 + 1)

    zg_sends = []
    for step in (4, 3, 5, 2, 6, 1, 7):
        offset = (NZ - step) % NZ
        side = 0 if offset in NEAR else 1
        slot = OFFSETS[side].index(offset) * 2 + core
        copy = remote(
            own32, zgather.at[slot], zg_send.at[step], zg_recv.at[slot], device(x, y, (z + step) % NZ, side)
        )
        copy.start()
        zg_sends.append(copy)
    to_core0 = remote(own32, zgather.at[1], zg_send.at[0], zg_recv.at[1], device(x, y, z, 0))

    @pl.when(core == 1)
    def _():
        to_core0.start()

    @pl.when(core == 0)
    def _():
        zgather[0] = own32[...]

    to_twin = (
        remote(limits.at[0], limits.at[1], archive_send.at[2], archive_recv.at[2], twin),
        remote(keys_hbm, keys.at[1], archive_send.at[0], archive_recv.at[0], twin),
        remote(futures_hbm, futures.at[1], archive_send.at[1], archive_recv.at[1], twin),
    )
    for copy in to_twin:
        copy.start()

    loads[2].wait()
    position = lax.broadcasted_iota(jnp.int32, (1, MINE), 1)
    lane = lax.broadcasted_iota(jnp.int32, (32, 128), 1)
    row = lax.broadcasted_iota(jnp.int32, (32, 128), 0)
    for group in range(2):
        wanted = natural_row(0, row // 8, group * 4 + (row // 2) % 4, core, row % 2)
        for block in range(NX):
            picked = jnp.where(lane == wanted, owners[block : block + 1, :].astype(jnp.float32), 0.0)
            owner = jnp.sum(picked, axis=1, keepdims=True)
            at = group * GROUP + block * 32
            for side in range(2):
                held = natural_row(
                    position // 64,
                    (position // 16) % 4,
                    (z + pick((position // 4) % 4, OFFSETS[side])) % NZ,
                    (position // 2) % 2,
                    position % 2,
                )
                onehot[side, at : at + 32, :] = jnp.where(
                    owner == held.astype(jnp.float32), 1.0, 0.0
                ).astype(jnp.bfloat16)

    def zg_wait(slot):
        remote(own32, zgather.at[slot], zg_send.at[0], zg_recv.at[slot], twin).wait_recv()

    for slot in range(1, 8):
        zg_wait(slot)

    @pl.when(core == 1)
    def _():
        zg_wait(0)

    for slot in range(8):
        gather32[2 * slot : 2 * slot + 2, :] = zgather[slot]
    gathered[core, plane] = gather32[...].astype(jnp.bfloat16)

    pg_sends = []
    for k, step in enumerate(STEPS):
        other, target = plane_peer(step)
        block = gathered.at[core, plane]
        copy = remote(block, block, pg_send.at[k], pg_recv.at[plane], target)
        copy.start()
        pg_sends.append(copy)

    def fw_copy(other):
        block = gathered.at[core, other]
        return remote(block, block, fw_send.at[other], fw_recv.at[other], twin)

    fw_copy(plane).start()
    for step in STEPS:
        other, target = plane_peer(step)
        block = gathered.at[core, other]
        remote(block, block, pg_send.at[0], pg_recv.at[other], target).wait_recv()
        fw_copy(other).start()

    every = gathered[core].reshape(MINE, WIDTH)
    mine = jnp.dot(onehot[core], every, preferred_element_type=jnp.float32)

    for load in loads[3:]:
        load.wait()
    for copy in to_twin:
        copy.wait()

    def fw_wait(other, carry):
        block = gathered.at[1 - core, other]
        remote(block, block, fw_send.at[other], fw_recv.at[other], twin).wait_recv()
        return carry

    lax.fori_loop(0, PLANE, fw_wait, 0)

    every = gathered[1 - core].reshape(MINE, WIDTH)
    mine = (mine + jnp.dot(onehot[1 - core], every, preferred_element_type=jnp.float32)).astype(jnp.bfloat16)

    column = lax.broadcasted_iota(jnp.int32, (1, TILE), 1).astype(jnp.float32)
    best = None
    for half in range(2):
        limit = limits[half, 0:1, 0:1]
        for tile in range(ARCHIVE // TILE):
            part = lax.dot_general(
                mine,
                keys[half, tile * TILE : (tile + 1) * TILE, :],
                (((1,), (1,)), ((), ())),
                preferred_element_type=jnp.float32,
            )
            if tile > 0:
                part = jnp.where(column + float(tile * TILE) < limit, part, -1e30)
            at = half * ARCHIVE + tile * TILE
            scores[:, at : at + TILE] = part
            top = jnp.max(part, axis=1, keepdims=True)
            best = top if best is None else jnp.maximum(best, top)
    total = jnp.zeros((MINE, 1), jnp.float32)
    for tile in range(2 * ARCHIVE // TILE):
        span = slice(tile * TILE, (tile + 1) * TILE)
        weight = jnp.exp2((scores[:, span] - best) * exponent_factor)
        weights[:, span] = weight.astype(jnp.bfloat16)
        total = total + jnp.sum(weight, axis=1, keepdims=True)

    stat_lane = lax.broadcasted_iota(jnp.int32, (MINE, STATS), 1)
    stat_row = lax.broadcasted_iota(jnp.int32, (MINE, STATS), 0)
    stat_here = stat_lane == (stat_row // GROUP) * 8 + stat_row % 8
    for k, value in enumerate((best, total)):
        value = jnp.where(stat_here, value, 0.0).reshape(2, PLANE, 8, STATS)
        stat_send[:, k : k + 1, :] = jnp.sum(value[0] + value[1], axis=1, keepdims=True)
    st_sends = []
    for k, step in enumerate(STEPS):
        other, target = plane_peer(step)
        copy = remote(stat_send.at[other], stat_recv.at[plane], st_send.at[k], st_recv.at[plane], target)
        copy.start()
        st_sends.append(copy)
    stat_recv[plane] = stat_send[plane]

    ps_sends = []
    for group, (send, recv) in enumerate(((low_send, low_recv), (high_send, high_recv))):
        halves = []
        for half in range(2):
            span = slice(half * HALF, (half + 1) * HALF)
            sums = None
            for side in range(2):
                term = jnp.dot(
                    weights[group * GROUP : (group + 1) * GROUP, side * ARCHIVE : (side + 1) * ARCHIVE],
                    futures[side, :, span],
                    preferred_element_type=jnp.float32,
                )
                sums = term if sums is None else sums + term
            halves.append(sums.reshape(PLANE, 8, HALF))
        sums = jnp.stack(halves, axis=1).reshape(MINE, HALF)
        send[...] = sums.astype(jnp.bfloat16).reshape(PLANE, ROWS, HALF)
        for k, step in enumerate(STEPS):
            other, target = plane_peer(step)
            copy = remote(send.at[other], recv.at[plane], ps_send.at[group, k], ps_recv.at[group, plane], target)
            copy.start()
            ps_sends.append(copy)
        recv[plane] = send[plane]

    for step in STEPS:
        other, target = plane_peer(step)
        remote(stat_send.at[other], stat_recv.at[other], st_send.at[0], st_recv.at[other], target).wait_recv()
    at_row = lax.broadcasted_iota(jnp.int32, (ROWS, STATS), 0) == lax.broadcasted_iota(jnp.int32, (ROWS, STATS), 1)

    def upright(value):
        return jnp.sum(jnp.where(at_row, value, 0.0), axis=1, keepdims=True)

    maxima = [stat_recv[k, 0:1, :] for k in range(PLANE)]
    best = maxima[0]
    for k in range(1, PLANE):
        best = jnp.maximum(best, maxima[k])
    scales = [jnp.exp2((m - best) * exponent_factor) for m in maxima]
    total = jnp.zeros((1, STATS), jnp.float32)
    for k in range(PLANE):
        total = total + stat_recv[k, 1:2, :] * scales[k]
    scales = [upright(scale) for scale in scales]
    passed_lane = lax.broadcasted_iota(jnp.int32, (1, STATS), 1)
    passed = jnp.where(passed_lane < 64, upright(best), upright(total))

    def zs_copy(group, step):
        other = group * 4 + (z + step) % 4
        return remote(
            zpart_send.at[other],
            zpart_recv.at[z],
            zs_send.at[other],
            zs_recv.at[z],
            device(x, y, other, core),
        )

    for group, (send, recv) in enumerate(((low_send, low_recv), (high_send, high_recv))):
        for step in STEPS:
            other, target = plane_peer(step)
            remote(send.at[other], recv.at[other], ps_send.at[group, 0], ps_recv.at[group, other], target).wait_recv()
        sums = jnp.zeros((ROWS, HALF), jnp.float32)
        for k in range(PLANE):
            scale = scales[k][group * 8 : group * 8 + 8]
            scale = jnp.concatenate([scale, scale], axis=0)
            sums = sums + recv[k].astype(jnp.float32) * scale
        for index in range(4):
            slot = group * 4 + index
            zpart_send[slot, :, :HALF] = sums[2 * index : 2 * index + 2, :]
            zpart_send[slot, :, HALF:WIDTH] = sums[8 + 2 * index : 8 + 2 * index + 2, :]
            zpart_send[slot, :, WIDTH:] = passed[group * 8 + 2 * index : group * 8 + 2 * index + 2, :]
        for step in range(3, 0, -1):
            zs_copy(group, step).start()

        @pl.when(z // 4 == group)
        def _():
            zpart_recv[z] = zpart_send[z]

        @pl.when(z // 4 != group)
        def _():
            zs_copy(group, 0).start()

    for step in range(1, NZ):
        other = (z + step) % NZ
        remote(zpart_send.at[0], zpart_recv.at[other], zs_send.at[0], zs_recv.at[other], twin).wait_recv()

    best = zpart_recv[0, :, WIDTH : WIDTH + 1]
    for k in range(1, NZ):
        best = jnp.maximum(best, zpart_recv[k, :, WIDTH : WIDTH + 1])
    sums = jnp.zeros((2, WIDTH), jnp.float32)
    total = jnp.zeros((2, 1), jnp.float32)
    for k in range(NZ):
        stats = zpart_recv[k, :, WIDTH:]
        scale = jnp.exp2((stats[:, 0:1] - best) * exponent_factor)
        sums = sums + zpart_recv[k, :, :WIDTH] * scale
        total = total + stats[:, 64:65] * scale
    analog = sums / total
    norm_factor = lax.rsqrt(jnp.mean(analog * analog, axis=1, keepdims=True) + 1e-06)
    out[...] = (analog * norm_factor).astype(jnp.bfloat16)

    for copy in zg_sends + pg_sends + st_sends + ps_sends:
        copy.wait_send()
    for group in range(2):
        for step in range(1, 4):
            zs_copy(group, step).wait_send()

        @pl.when(z // 4 != group)
        def _():
            zs_copy(group, 0).wait_send()

    @pl.when(core == 1)
    def _():
        to_core0.wait_send()

    def fw_sent(other, carry):
        fw_copy(other).wait_send()
        return carry

    lax.fori_loop(0, PLANE, fw_sent, 0)


def in_hbm(array):
    return pltpu.with_memory_space_constraint(array, pltpu.HBM)


def body(queries, archive_keys, futures, counts, owners):
    hbm = pl.BlockSpec(memory_space=pltpu.HBM)
    dma = pltpu.SemaphoreType.DMA
    bf16, f32 = jnp.bfloat16, jnp.float32
    return pl.pallas_call(
        kernel,
        out_shape=jax.ShapeDtypeStruct((2, WIDTH), bf16),
        in_specs=[hbm] * 5,
        out_specs=pl.BlockSpec(memory_space=pltpu.VMEM),
        scratch_shapes=[
            pltpu.VMEM((2, WIDTH), bf16),
            pltpu.SMEM((1,), jnp.int32),
            pltpu.VMEM((4, 128), jnp.int32),
            pltpu.VMEM((2, WIDTH), f32),
            pltpu.VMEM((8, 2, WIDTH), f32),
            pltpu.VMEM((ROWS, WIDTH), f32),
            pltpu.VMEM((2, PLANE, ROWS, WIDTH), bf16),
            pltpu.VMEM((2, ARCHIVE, WIDTH), bf16),
            pltpu.VMEM((2, ARCHIVE, WIDTH), bf16),
            pltpu.VMEM((2, 8, 128), f32),
            pltpu.VMEM((2, MINE, MINE), bf16),
            pltpu.VMEM((MINE, 2 * ARCHIVE), f32),
            pltpu.VMEM((MINE, 2 * ARCHIVE), bf16),
            pltpu.VMEM((PLANE, ROWS, HALF), bf16),
            pltpu.VMEM((PLANE, ROWS, HALF), bf16),
            pltpu.VMEM((PLANE, ROWS, HALF), bf16),
            pltpu.VMEM((PLANE, ROWS, HALF), bf16),
            pltpu.VMEM((PLANE, 2, STATS), f32),
            pltpu.VMEM((PLANE, 2, STATS), f32),
            pltpu.VMEM((NZ, 2, WIDTH + STATS), f32),
            pltpu.VMEM((NZ, 2, WIDTH + STATS), f32),
            dma((5,)),
            dma((3,)),
            dma((3,)),
            dma((NZ,)),
            dma((NZ,)),
            dma((PLANE,)),
            dma((PLANE,)),
            dma((PLANE,)),
            dma((PLANE,)),
            dma((2, PLANE)),
            dma((2, PLANE)),
            dma((PLANE,)),
            dma((PLANE,)),
            dma((NZ,)),
            dma((NZ,)),
        ],
        compiler_params=pltpu.CompilerParams(
            collective_id=0, has_side_effects=True, vmem_limit_bytes=40 * 2**20
        ),
        name="analog_forecast",
    )(in_hbm(queries), in_hbm(archive_keys), in_hbm(futures), counts, in_hbm(owners.reshape(4, 128)))


def solution(mesh):
    rows = P(("wide", "narrow"), None)
    return jax.shard_map(
        body,
        mesh=mesh,
        in_specs=(rows, rows, rows, P(("wide", "narrow")), P()),
        out_specs=rows,
        check_vma=False,
    )
```

```python
import jax
import jax.numpy as jnp
from jax import lax
from jax.experimental import pallas as pl
from jax.experimental.pallas import tpu as pltpu
from jax.sharding import PartitionSpec as P

MESH = pl.DeviceIdType.MESH

NX, NY, NZ = 4, 4, 8
PLANE = NX * NY
ROWS = 16
MINE = PLANE * ROWS
GROUP = MINE // 2
WIDTH = 1024
HALF = 512
STATS = 128
ARCHIVE = 768
TILE = 256

NEAR, FAR = (0, 1, 7, 6), (4, 3, 5, 2)
OFFSETS = NEAR, FAR

STEPS = sorted(
    [(a, b) for a in range(NX) for b in range(NY) if a or b],
    key=lambda s: -(min(s[0], NX - s[0]) + min(s[1], NY - s[1])),
)

score_scale = 3.0
exponent_factor = score_scale / 32.0 * 1.4426950408889634


def pick(index, values):
    result = jnp.full_like(index, values[0])
    for k in range(1, len(values)):
        result = jnp.where(index == k, values[k], result)
    return result


def natural_row(x, y, z, core, row):
    return x * 128 + z * 16 + core * 8 + y * 2 + row


def kernel(
    queries_hbm,
    keys_hbm,
    futures_hbm,
    counts_hbm,
    owners_hbm,
    out,
    queries,
    counts,
    owners,
    own32,
    zgather,
    gather32,
    gathered,
    keys,
    upright_keys,
    futures,
    limits,
    onehot,
    scores,
    weights,
    low_send,
    low_recv,
    high_send,
    high_recv,
    stat_send,
    stat_recv,
    zpart_send,
    zpart_recv,
    local_sem,
    archive_send,
    archive_recv,
    zg_send,
    zg_recv,
    pg_send,
    pg_recv,
    fw_send,
    fw_recv,
    ps_send,
    ps_recv,
    st_send,
    st_recv,
    zs_send,
    zs_recv,
):
    wide, y = lax.axis_index("wide"), lax.axis_index("narrow")
    x, z, core = wide // 16, (wide // 2) % 8, wide % 2
    plane = x * NY + y

    def device(x, y, z, core):
        return {"wide": (x * NZ + z) * 2 + core, "narrow": y}

    def plane_peer(step):
        other_x, other_y = (x + step[0]) % NX, (y + step[1]) % NY
        return other_x * NY + other_y, device(other_x, other_y, z, core)

    twin = device(x, y, z, 1 - core)

    def remote(src, dst, send, recv, target):
        return pltpu.make_async_remote_copy(
            src_ref=src, dst_ref=dst, send_sem=send, recv_sem=recv, device_id=target, device_id_type=MESH
        )

    loads = [
        pltpu.make_async_copy(src, dst, local_sem.at[k])
        for k, (src, dst) in enumerate(
            [
                (queries_hbm, queries),
                (counts_hbm, counts),
                (owners_hbm, owners),
                (keys_hbm, keys.at[0]),
                (futures_hbm, futures.at[0]),
            ]
        )
    ]
    loads[0].start()
    loads[1].start()

    barrier = pltpu.get_barrier_semaphore()
    for step in (4, 3, 5, 2, 6, 1, 7):
        for side in range(2):
            pl.semaphore_signal(
                barrier, inc=1, device_id=device(x, y, (z + step) % NZ, side), device_id_type=MESH
            )
    for step in STEPS:
        pl.semaphore_signal(barrier, inc=1, device_id=plane_peer(step)[1], device_id_type=MESH)
    pl.semaphore_signal(barrier, inc=1, device_id=twin, device_id_type=MESH)
    for load in loads[2:]:
        load.start()
    loads[0].wait()
    own32[...] = queries[...].astype(jnp.float32)
    loads[1].wait()
    limits[0] = jnp.full((8, 128), counts[0], jnp.int32).astype(jnp.float32)
    pl.semaphore_wait(barrier, 2 * (NZ - 1) + PLANE - 1 + 1)

    zg_sends = []
    for step in (4, 3, 5, 2, 6, 1, 7):
        offset = (NZ - step) % NZ
        side = 0 if offset in NEAR else 1
        slot = OFFSETS[side].index(offset) * 2 + core
        copy = remote(
            own32, zgather.at[slot], zg_send.at[step], zg_recv.at[slot], device(x, y, (z + step) % NZ, side)
        )
        copy.start()
        zg_sends.append(copy)
    to_core0 = remote(own32, zgather.at[1], zg_send.at[0], zg_recv.at[1], device(x, y, z, 0))

    @pl.when(core == 1)
    def _():
        to_core0.start()

    @pl.when(core == 0)
    def _():
        zgather[0] = own32[...]

    to_twin = (
        remote(limits.at[0], limits.at[1], archive_send.at[2], archive_recv.at[2], twin),
        remote(keys_hbm, keys.at[1], archive_send.at[0], archive_recv.at[0], twin),
        remote(futures_hbm, futures.at[1], archive_send.at[1], archive_recv.at[1], twin),
    )
    for copy in to_twin:
        copy.start()

    loads[2].wait()
    position = lax.broadcasted_iota(jnp.int32, (1, MINE), 1)
    lane = lax.broadcasted_iota(jnp.int32, (32, 128), 1)
    row = lax.broadcasted_iota(jnp.int32, (32, 128), 0)
    for group in range(2):
        wanted = natural_row(0, row // 8, group * 4 + (row // 2) % 4, core, row % 2)
        for block in range(NX):
            picked = jnp.where(lane == wanted, owners[block : block + 1, :].astype(jnp.float32), 0.0)
            owner = jnp.sum(picked, axis=1, keepdims=True)
            at = group * GROUP + block * 32
            for side in range(2):
                held = natural_row(
                    position // 64,
                    (position // 16) % 4,
                    (z + pick((position // 4) % 4, OFFSETS[side])) % NZ,
                    (position // 2) % 2,
                    position % 2,
                )
                onehot[side, at : at + 32, :] = jnp.where(
                    owner == held.astype(jnp.float32), 1.0, 0.0
                ).astype(jnp.bfloat16)

    def turn_keys(side):
        for tile in range(ARCHIVE // TILE):
            at = side * ARCHIVE + tile * TILE
            upright_keys[:, at : at + TILE] = keys[side, tile * TILE : (tile + 1) * TILE, :].T

    loads[3].wait()
    turn_keys(0)

    def zg_wait(slot):
        remote(own32, zgather.at[slot], zg_send.at[0], zg_recv.at[slot], twin).wait_recv()

    for slot in range(1, 8):
        zg_wait(slot)

    @pl.when(core == 1)
    def _():
        zg_wait(0)

    for slot in range(8):
        gather32[2 * slot : 2 * slot + 2, :] = zgather[slot]
    gathered[core, plane] = gather32[...].astype(jnp.bfloat16)

    pg_sends = []
    for k, step in enumerate(STEPS):
        other, target = plane_peer(step)
        block = gathered.at[core, plane]
        copy = remote(block, block, pg_send.at[k], pg_recv.at[plane], target)
        copy.start()
        pg_sends.append(copy)

    def fw_copy(other):
        block = gathered.at[core, other]
        return remote(block, block, fw_send.at[other], fw_recv.at[other], twin)

    fw_copy(plane).start()
    loads[4].wait()
    for copy in to_twin:
        copy.wait()
    turn_keys(1)
    for step in STEPS:
        other, target = plane_peer(step)
        block = gathered.at[core, other]
        remote(block, block, pg_send.at[0], pg_recv.at[other], target).wait_recv()
        fw_copy(other).start()

    every = gathered[core].reshape(MINE, WIDTH)
    mine = jnp.dot(onehot[core], every, preferred_element_type=jnp.float32)


    def fw_wait(other, carry):
        block = gathered.at[1 - core, other]
        remote(block, block, fw_send.at[other], fw_recv.at[other], twin).wait_recv()
        return carry

    lax.fori_loop(0, PLANE, fw_wait, 0)

    every = gathered[1 - core].reshape(MINE, WIDTH)
    mine = (mine + jnp.dot(onehot[1 - core], every, preferred_element_type=jnp.float32)).astype(jnp.bfloat16)

    column = lax.broadcasted_iota(jnp.int32, (1, TILE), 1).astype(jnp.float32)
    def score(group):
        for side in range(2):
            limit = limits[side, 0:1, 0:1]
            for tile in range(ARCHIVE // TILE):
                at = side * ARCHIVE + tile * TILE
                part = jnp.dot(
                    mine[group * GROUP : (group + 1) * GROUP],
                    upright_keys[:, at : at + TILE],
                    preferred_element_type=jnp.float32,
                )
                if tile > 0:
                    part = jnp.where(column + float(tile * TILE) < limit, part, -1e30)
                scores[group, :, at : at + TILE] = part

    def softmax(group):
        best = None
        for tile in range(2 * ARCHIVE // TILE):
            top = jnp.max(scores[group, :, tile * TILE : (tile + 1) * TILE], axis=1, keepdims=True)
            best = top if best is None else jnp.maximum(best, top)
        total = jnp.zeros((GROUP, 1), jnp.float32)
        for tile in range(2 * ARCHIVE // TILE):
            span = slice(tile * TILE, (tile + 1) * TILE)
            weight = jnp.exp2((scores[group, :, span] - best) * exponent_factor)
            weights[group, :, span] = weight.astype(jnp.bfloat16)
            total = total + jnp.sum(weight, axis=1, keepdims=True)
        return best, total

    here = lax.broadcasted_iota(jnp.int32, (GROUP, STATS), 0) % 8 == lax.broadcasted_iota(jnp.int32, (GROUP, STATS), 1)
    ps_sends, st_sends = [], []
    for group, (send, recv) in enumerate(((low_send, low_recv), (high_send, high_recv))):
        score(group)
        for k, value in enumerate(softmax(group)):
            value = jnp.where(here, value, 0.0).reshape(PLANE, 8, STATS)
            stat_send[group, :, k : k + 1, :] = jnp.sum(value, axis=1, keepdims=True)
        for k, step in enumerate(STEPS):
            other, target = plane_peer(step)
            copy = remote(
                stat_send.at[group, other],
                stat_recv.at[group, plane],
                st_send.at[group, k],
                st_recv.at[group, plane],
                target,
            )
            copy.start()
            st_sends.append(copy)
        stat_recv[group, plane] = stat_send[group, plane]
        halves = []
        for half in range(2):
            span = slice(half * HALF, (half + 1) * HALF)
            sums = None
            for side in range(2):
                term = jnp.dot(
                    weights[group, :, side * ARCHIVE : (side + 1) * ARCHIVE],
                    futures[side, :, span],
                    preferred_element_type=jnp.float32,
                )
                sums = term if sums is None else sums + term
            halves.append(sums.reshape(PLANE, 8, HALF))
        sums = jnp.stack(halves, axis=1).reshape(MINE, HALF)
        send[...] = sums.astype(jnp.bfloat16).reshape(PLANE, ROWS, HALF)
        for k, step in enumerate(STEPS):
            other, target = plane_peer(step)
            copy = remote(send.at[other], recv.at[plane], ps_send.at[group, k], ps_recv.at[group, plane], target)
            copy.start()
            ps_sends.append(copy)
        recv[plane] = send[plane]

    for copy in zg_sends + pg_sends:
        copy.wait_send()

    @pl.when(core == 1)
    def _():
        to_core0.wait_send()

    def fw_sent(other, carry):
        fw_copy(other).wait_send()
        return carry

    lax.fori_loop(0, PLANE, fw_sent, 0)

    at_row = lax.broadcasted_iota(jnp.int32, (8, STATS), 0) == lax.broadcasted_iota(jnp.int32, (8, STATS), 1)

    def upright(value):
        return jnp.sum(jnp.where(at_row, value, 0.0), axis=1, keepdims=True)

    passed_lane = lax.broadcasted_iota(jnp.int32, (1, STATS), 1)
    def zs_copy(group, step):
        other = group * 4 + (z + step) % 4
        return remote(
            zpart_send.at[other],
            zpart_recv.at[z],
            zs_send.at[other],
            zs_recv.at[z],
            device(x, y, other, core),
        )

    for group, (send, recv) in enumerate(((low_send, low_recv), (high_send, high_recv))):
        for step in STEPS:
            other, target = plane_peer(step)
            remote(
                stat_send.at[group, other],
                stat_recv.at[group, other],
                st_send.at[group, 0],
                st_recv.at[group, other],
                target,
            ).wait_recv()
        maxima = [stat_recv[group, k, 0:1, :] for k in range(PLANE)]
        best = maxima[0]
        for k in range(1, PLANE):
            best = jnp.maximum(best, maxima[k])
        scales = [jnp.exp2((m - best) * exponent_factor) for m in maxima]
        total = jnp.zeros((1, STATS), jnp.float32)
        for k in range(PLANE):
            total = total + stat_recv[group, k, 1:2, :] * scales[k]
        scales = [upright(scale) for scale in scales]
        passed = jnp.where(passed_lane < 64, upright(best), upright(total))
        for step in STEPS:
            other, target = plane_peer(step)
            remote(send.at[other], recv.at[other], ps_send.at[group, 0], ps_recv.at[group, other], target).wait_recv()
        sums = jnp.zeros((ROWS, HALF), jnp.float32)
        for k in range(PLANE):
            scale = jnp.concatenate([scales[k], scales[k]], axis=0)
            sums = sums + recv[k].astype(jnp.float32) * scale
        for index in range(4):
            slot = group * 4 + index
            zpart_send[slot, :, :HALF] = sums[2 * index : 2 * index + 2, :]
            zpart_send[slot, :, HALF:WIDTH] = sums[8 + 2 * index : 8 + 2 * index + 2, :]
            zpart_send[slot, :, WIDTH:] = passed[2 * index : 2 * index + 2, :]
        for step in range(3, 0, -1):
            zs_copy(group, step).start()

        @pl.when(z // 4 == group)
        def _():
            zpart_recv[z] = zpart_send[z]

        @pl.when(z // 4 != group)
        def _():
            zs_copy(group, 0).start()

    for copy in st_sends + ps_sends:
        copy.wait_send()

    for step in range(1, NZ):
        other = (z + step) % NZ
        remote(zpart_send.at[0], zpart_recv.at[other], zs_send.at[0], zs_recv.at[other], twin).wait_recv()

    best = zpart_recv[0, :, WIDTH : WIDTH + 1]
    for k in range(1, NZ):
        best = jnp.maximum(best, zpart_recv[k, :, WIDTH : WIDTH + 1])
    sums = jnp.zeros((2, WIDTH), jnp.float32)
    total = jnp.zeros((2, 1), jnp.float32)
    for k in range(NZ):
        stats = zpart_recv[k, :, WIDTH:]
        scale = jnp.exp2((stats[:, 0:1] - best) * exponent_factor)
        sums = sums + zpart_recv[k, :, :WIDTH] * scale
        total = total + stats[:, 64:65] * scale
    analog = sums / total
    norm_factor = lax.rsqrt(jnp.mean(analog * analog, axis=1, keepdims=True) + 1e-06)
    out[...] = (analog * norm_factor).astype(jnp.bfloat16)

    for group in range(2):
        for step in range(1, 4):
            zs_copy(group, step).wait_send()

        @pl.when(z // 4 != group)
        def _():
            zs_copy(group, 0).wait_send()


def in_hbm(array):
    return pltpu.with_memory_space_constraint(array, pltpu.HBM)


def body(queries, archive_keys, futures, counts, owners):
    hbm = pl.BlockSpec(memory_space=pltpu.HBM)
    dma = pltpu.SemaphoreType.DMA
    bf16, f32 = jnp.bfloat16, jnp.float32
    return pl.pallas_call(
        kernel,
        out_shape=jax.ShapeDtypeStruct((2, WIDTH), bf16),
        in_specs=[hbm] * 5,
        out_specs=pl.BlockSpec(memory_space=pltpu.VMEM),
        scratch_shapes=[
            pltpu.VMEM((2, WIDTH), bf16),
            pltpu.SMEM((1,), jnp.int32),
            pltpu.VMEM((4, 128), jnp.int32),
            pltpu.VMEM((2, WIDTH), f32),
            pltpu.VMEM((8, 2, WIDTH), f32),
            pltpu.VMEM((ROWS, WIDTH), f32),
            pltpu.VMEM((2, PLANE, ROWS, WIDTH), bf16),
            pltpu.VMEM((2, ARCHIVE, WIDTH), bf16),
            pltpu.VMEM((WIDTH, 2 * ARCHIVE), bf16),
            pltpu.VMEM((2, ARCHIVE, WIDTH), bf16),
            pltpu.VMEM((2, 8, 128), f32),
            pltpu.VMEM((2, MINE, MINE), bf16),
            pltpu.VMEM((2, GROUP, 2 * ARCHIVE), f32),
            pltpu.VMEM((2, GROUP, 2 * ARCHIVE), bf16),
            pltpu.VMEM((PLANE, ROWS, HALF), bf16),
            pltpu.VMEM((PLANE, ROWS, HALF), bf16),
            pltpu.VMEM((PLANE, ROWS, HALF), bf16),
            pltpu.VMEM((PLANE, ROWS, HALF), bf16),
            pltpu.VMEM((2, PLANE, 2, STATS), f32),
            pltpu.VMEM((2, PLANE, 2, STATS), f32),
            pltpu.VMEM((NZ, 2, WIDTH + STATS), f32),
            pltpu.VMEM((NZ, 2, WIDTH + STATS), f32),
            dma((5,)),
            dma((3,)),
            dma((3,)),
            dma((NZ,)),
            dma((NZ,)),
            dma((PLANE,)),
            dma((PLANE,)),
            dma((PLANE,)),
            dma((PLANE,)),
            dma((2, PLANE)),
            dma((2, PLANE)),
            dma((2, PLANE)),
            dma((2, PLANE)),
            dma((NZ,)),
            dma((NZ,)),
        ],
        compiler_params=pltpu.CompilerParams(
            collective_id=0, has_side_effects=True, vmem_limit_bytes=40 * 2**20
        ),
        name="analog_forecast",
    )(in_hbm(queries), in_hbm(archive_keys), in_hbm(futures), counts, in_hbm(owners.reshape(4, 128)))


def solution(mesh):
    rows = P(("wide", "narrow"), None)
    return jax.shard_map(
        body,
        mesh=mesh,
        in_specs=(rows, rows, rows, P(("wide", "narrow")), P()),
        out_specs=rows,
        check_vma=False,
    )
```

```python
import jax
import jax.numpy as jnp
from jax import lax
from jax.experimental import pallas as pl
from jax.experimental.pallas import tpu as pltpu
from jax.sharding import PartitionSpec as P

MESH = pl.DeviceIdType.MESH

NX, NY, NZ = 4, 4, 8
PLANE = NX * NY
ROWS = 16
MINE = PLANE * ROWS
GROUP = MINE // 2
WIDTH = 1024
HALF = 512
STATS = 128
ARCHIVE = 768
TILE = 256

OFFSETS = (0, 1, 2, 3), (4, 5, 6, 7)

STEPS = sorted(
    [(a, b) for a in range(NX) for b in range(NY) if a or b],
    key=lambda s: -(min(s[0], NX - s[0]) + min(s[1], NY - s[1])),
)

score_scale = 3.0
exponent_factor = score_scale / 32.0 * 1.4426950408889634


def pick(index, values):
    result = jnp.full_like(index, values[0])
    for k in range(1, len(values)):
        result = jnp.where(index == k, values[k], result)
    return result


def natural_row(x, y, z, core, row):
    return x * 128 + z * 16 + core * 8 + y * 2 + row


def kernel(
    queries_hbm,
    keys_hbm,
    futures_hbm,
    counts_hbm,
    owners_hbm,
    out,
    queries,
    counts,
    owners,
    own32,
    zgather,
    gather32,
    gathered,
    keys,
    upright_keys,
    futures,
    limits,
    onehot,
    scores,
    weights,
    low_send,
    low_recv,
    high_send,
    high_recv,
    stat_send,
    stat_recv,
    zpart_send,
    zpart_recv,
    local_sem,
    archive_send,
    archive_recv,
    zg_send,
    zg_recv,
    pg_send,
    pg_recv,
    fw_send,
    fw_recv,
    ps_send,
    ps_recv,
    st_send,
    st_recv,
    zs_send,
    zs_recv,
):
    wide, y = lax.axis_index("wide"), lax.axis_index("narrow")
    x, z, core = wide // 16, (wide // 2) % 8, wide % 2
    plane = x * NY + y

    def device(x, y, z, core):
        return {"wide": (x * NZ + z) * 2 + core, "narrow": y}

    def plane_peer(step):
        other_x, other_y = (x + step[0]) % NX, (y + step[1]) % NY
        return other_x * NY + other_y, device(other_x, other_y, z, core)

    twin = device(x, y, z, 1 - core)

    def remote(src, dst, send, recv, target):
        return pltpu.make_async_remote_copy(
            src_ref=src, dst_ref=dst, send_sem=send, recv_sem=recv, device_id=target, device_id_type=MESH
        )

    loads = [
        pltpu.make_async_copy(src, dst, local_sem.at[k])
        for k, (src, dst) in enumerate(
            [
                (queries_hbm, queries),
                (counts_hbm, counts),
                (owners_hbm, owners),
                (keys_hbm, keys.at[0]),
                (futures_hbm, futures.at[0]),
            ]
        )
    ]
    loads[0].start()
    loads[1].start()

    barrier = pltpu.get_barrier_semaphore()
    for step in (4, 3, 5, 2, 6, 1, 7):
        for side in range(2):
            pl.semaphore_signal(
                barrier, inc=1, device_id=device(x, y, (z + step) % NZ, side), device_id_type=MESH
            )
    for step in STEPS:
        pl.semaphore_signal(barrier, inc=1, device_id=plane_peer(step)[1], device_id_type=MESH)
    pl.semaphore_signal(barrier, inc=1, device_id=twin, device_id_type=MESH)
    for load in loads[2:]:
        load.start()
    loads[0].wait()
    own32[...] = queries[...].astype(jnp.float32)
    loads[1].wait()
    limits[0] = jnp.full((8, 128), counts[0], jnp.int32).astype(jnp.float32)
    pl.semaphore_wait(barrier, 2 * (NZ - 1) + PLANE - 1 + 1)

    zg_sends = []
    for step in (4, 3, 5, 2, 6, 1, 7):
        offset = (NZ - step) % NZ
        side = 0 if offset in OFFSETS[0] else 1
        slot = OFFSETS[side].index(offset) * 2 + core
        copy = remote(
            own32, zgather.at[slot], zg_send.at[step], zg_recv.at[slot], device(x, y, (z + step) % NZ, side)
        )
        copy.start()
        zg_sends.append(copy)
    to_core0 = remote(own32, zgather.at[1], zg_send.at[0], zg_recv.at[1], device(x, y, z, 0))

    @pl.when(core == 1)
    def _():
        to_core0.start()

    @pl.when(core == 0)
    def _():
        zgather[0] = own32[...]

    to_twin = (
        remote(limits.at[0], limits.at[1], archive_send.at[2], archive_recv.at[2], twin),
        remote(keys_hbm, keys.at[1], archive_send.at[0], archive_recv.at[0], twin),
        remote(futures_hbm, futures.at[1], archive_send.at[1], archive_recv.at[1], twin),
    )
    for copy in to_twin:
        copy.start()

    loads[2].wait()
    position = lax.broadcasted_iota(jnp.int32, (1, MINE), 1)
    lane = lax.broadcasted_iota(jnp.int32, (32, 128), 1)
    row = lax.broadcasted_iota(jnp.int32, (32, 128), 0)
    for group in range(2):
        wanted = natural_row(0, row // 8, group * 4 + (row // 2) % 4, core, row % 2)
        for block in range(NX):
            picked = jnp.where(lane == wanted, owners[block : block + 1, :].astype(jnp.float32), 0.0)
            owner = jnp.sum(picked, axis=1, keepdims=True)
            at = group * GROUP + block * 32
            for side in range(2):
                held = natural_row(
                    position // 64,
                    (position // 16) % 4,
                    (z + pick((position // 4) % 4, OFFSETS[side])) % NZ,
                    (position // 2) % 2,
                    position % 2,
                )
                onehot[side, at : at + 32, :] = jnp.where(
                    owner == held.astype(jnp.float32), 1.0, 0.0
                ).astype(jnp.bfloat16)

    def turn_keys(side):
        for tile in range(ARCHIVE // TILE):
            at = side * ARCHIVE + tile * TILE
            upright_keys[:, at : at + TILE] = keys[side, tile * TILE : (tile + 1) * TILE, :].T

    loads[3].wait()
    turn_keys(0)

    def zg_wait(slot):
        remote(own32, zgather.at[slot], zg_send.at[0], zg_recv.at[slot], twin).wait_recv()

    for slot in range(1, 8):
        zg_wait(slot)

    @pl.when(core == 1)
    def _():
        zg_wait(0)

    for slot in range(8):
        gather32[2 * slot : 2 * slot + 2, :] = zgather[slot]
    gathered[core, plane] = gather32[...].astype(jnp.bfloat16)

    pg_sends = []
    for k, step in enumerate(STEPS):
        other, target = plane_peer(step)
        block = gathered.at[core, plane]
        copy = remote(block, block, pg_send.at[k], pg_recv.at[plane], target)
        copy.start()
        pg_sends.append(copy)

    def fw_copy(other):
        block = gathered.at[core, other]
        return remote(block, block, fw_send.at[other], fw_recv.at[other], twin)

    fw_copy(plane).start()
    loads[4].wait()
    for copy in to_twin:
        copy.wait()
    turn_keys(1)
    for step in STEPS:
        other, target = plane_peer(step)
        block = gathered.at[core, other]
        remote(block, block, pg_send.at[0], pg_recv.at[other], target).wait_recv()
        fw_copy(other).start()

    every = gathered[core].reshape(MINE, WIDTH)
    mine = jnp.dot(onehot[core], every, preferred_element_type=jnp.float32)


    def fw_wait(other, carry):
        block = gathered.at[1 - core, other]
        remote(block, block, fw_send.at[other], fw_recv.at[other], twin).wait_recv()
        return carry

    lax.fori_loop(0, PLANE, fw_wait, 0)

    every = gathered[1 - core].reshape(MINE, WIDTH)
    mine = (mine + jnp.dot(onehot[1 - core], every, preferred_element_type=jnp.float32)).astype(jnp.bfloat16)

    column = lax.broadcasted_iota(jnp.int32, (1, TILE), 1).astype(jnp.float32)
    def score(group):
        for side in range(2):
            limit = limits[side, 0:1, 0:1]
            for tile in range(ARCHIVE // TILE):
                at = side * ARCHIVE + tile * TILE
                part = jnp.dot(
                    mine[group * GROUP : (group + 1) * GROUP],
                    upright_keys[:, at : at + TILE],
                    preferred_element_type=jnp.float32,
                )
                if tile > 0:
                    part = jnp.where(column + float(tile * TILE) < limit, part, -1e30)
                scores[group, :, at : at + TILE] = part

    def softmax(group):
        best = None
        for tile in range(2 * ARCHIVE // TILE):
            top = jnp.max(scores[group, :, tile * TILE : (tile + 1) * TILE], axis=1, keepdims=True)
            best = top if best is None else jnp.maximum(best, top)
        total = jnp.zeros((GROUP, 1), jnp.float32)
        for tile in range(2 * ARCHIVE // TILE):
            span = slice(tile * TILE, (tile + 1) * TILE)
            weight = jnp.exp2((scores[group, :, span] - best) * exponent_factor)
            weights[group, :, span] = weight.astype(jnp.bfloat16)
            total = total + jnp.sum(weight, axis=1, keepdims=True)
        return best, total

    here = lax.broadcasted_iota(jnp.int32, (GROUP, STATS), 0) % 8 == lax.broadcasted_iota(jnp.int32, (GROUP, STATS), 1)
    ps_sends, st_sends = [], []
    for group, (send, recv) in enumerate(((low_send, low_recv), (high_send, high_recv))):
        score(group)
        for k, value in enumerate(softmax(group)):
            value = jnp.where(here, value, 0.0).reshape(PLANE, 8, STATS)
            stat_send[group, :, k : k + 1, :] = jnp.sum(value, axis=1, keepdims=True)
        for k, step in enumerate(STEPS):
            other, target = plane_peer(step)
            copy = remote(
                stat_send.at[group, other],
                stat_recv.at[group, plane],
                st_send.at[group, k],
                st_recv.at[group, plane],
                target,
            )
            copy.start()
            st_sends.append(copy)
        stat_recv[group, plane] = stat_send[group, plane]
        halves = []
        for half in range(2):
            span = slice(half * HALF, (half + 1) * HALF)
            sums = None
            for side in range(2):
                term = jnp.dot(
                    weights[group, :, side * ARCHIVE : (side + 1) * ARCHIVE],
                    futures[side, :, span],
                    preferred_element_type=jnp.float32,
                )
                sums = term if sums is None else sums + term
            halves.append(sums.reshape(PLANE, 8, HALF))
        sums = jnp.stack(halves, axis=1).reshape(MINE, HALF)
        send[...] = sums.astype(jnp.bfloat16).reshape(PLANE, ROWS, HALF)
        for k, step in enumerate(STEPS):
            other, target = plane_peer(step)
            copy = remote(send.at[other], recv.at[plane], ps_send.at[group, k], ps_recv.at[group, plane], target)
            copy.start()
            ps_sends.append(copy)
        recv[plane] = send[plane]

    for copy in zg_sends + pg_sends:
        copy.wait_send()

    @pl.when(core == 1)
    def _():
        to_core0.wait_send()

    def fw_sent(other, carry):
        fw_copy(other).wait_send()
        return carry

    lax.fori_loop(0, PLANE, fw_sent, 0)

    at_row = lax.broadcasted_iota(jnp.int32, (8, STATS), 0) == lax.broadcasted_iota(jnp.int32, (8, STATS), 1)

    def upright(value):
        return jnp.sum(jnp.where(at_row, value, 0.0), axis=1, keepdims=True)

    passed_lane = lax.broadcasted_iota(jnp.int32, (1, STATS), 1)
    def zs_copy(group, step):
        other = group * 4 + (z + step) % 4
        return remote(
            zpart_send.at[other],
            zpart_recv.at[z],
            zs_send.at[other],
            zs_recv.at[z],
            device(x, y, other, core),
        )

    for group, (send, recv) in enumerate(((low_send, low_recv), (high_send, high_recv))):
        for step in STEPS:
            other, target = plane_peer(step)
            remote(
                stat_send.at[group, other],
                stat_recv.at[group, other],
                st_send.at[group, 0],
                st_recv.at[group, other],
                target,
            ).wait_recv()
        maxima = [stat_recv[group, k, 0:1, :] for k in range(PLANE)]
        best = maxima[0]
        for k in range(1, PLANE):
            best = jnp.maximum(best, maxima[k])
        scales = [jnp.exp2((m - best) * exponent_factor) for m in maxima]
        total = jnp.zeros((1, STATS), jnp.float32)
        for k in range(PLANE):
            total = total + stat_recv[group, k, 1:2, :] * scales[k]
        scales = [upright(scale) for scale in scales]
        passed = jnp.where(passed_lane < 64, upright(best), upright(total))
        for step in STEPS:
            other, target = plane_peer(step)
            remote(send.at[other], recv.at[other], ps_send.at[group, 0], ps_recv.at[group, other], target).wait_recv()
        sums = jnp.zeros((ROWS, HALF), jnp.float32)
        for k in range(PLANE):
            scale = jnp.concatenate([scales[k], scales[k]], axis=0)
            sums = sums + recv[k].astype(jnp.float32) * scale
        for index in range(4):
            slot = group * 4 + index
            zpart_send[slot, :, :HALF] = sums[2 * index : 2 * index + 2, :]
            zpart_send[slot, :, HALF:WIDTH] = sums[8 + 2 * index : 8 + 2 * index + 2, :]
            zpart_send[slot, :, WIDTH:] = passed[2 * index : 2 * index + 2, :]
        for step in range(3, 0, -1):
            zs_copy(group, step).start()

        @pl.when(z // 4 == group)
        def _():
            zpart_recv[z] = zpart_send[z]

        @pl.when(z // 4 != group)
        def _():
            zs_copy(group, 0).start()

    for copy in st_sends + ps_sends:
        copy.wait_send()

    for step in range(1, NZ):
        other = (z + step) % NZ
        remote(zpart_send.at[0], zpart_recv.at[other], zs_send.at[0], zs_recv.at[other], twin).wait_recv()

    best = zpart_recv[0, :, WIDTH : WIDTH + 1]
    for k in range(1, NZ):
        best = jnp.maximum(best, zpart_recv[k, :, WIDTH : WIDTH + 1])
    sums = jnp.zeros((2, WIDTH), jnp.float32)
    total = jnp.zeros((2, 1), jnp.float32)
    for k in range(NZ):
        stats = zpart_recv[k, :, WIDTH:]
        scale = jnp.exp2((stats[:, 0:1] - best) * exponent_factor)
        sums = sums + zpart_recv[k, :, :WIDTH] * scale
        total = total + stats[:, 64:65] * scale
    analog = sums / total
    norm_factor = lax.rsqrt(jnp.mean(analog * analog, axis=1, keepdims=True) + 1e-06)
    out[...] = (analog * norm_factor).astype(jnp.bfloat16)

    for group in range(2):
        for step in range(1, 4):
            zs_copy(group, step).wait_send()

        @pl.when(z // 4 != group)
        def _():
            zs_copy(group, 0).wait_send()


def in_hbm(array):
    return pltpu.with_memory_space_constraint(array, pltpu.HBM)


def body(queries, archive_keys, futures, counts, owners):
    hbm = pl.BlockSpec(memory_space=pltpu.HBM)
    dma = pltpu.SemaphoreType.DMA
    bf16, f32 = jnp.bfloat16, jnp.float32
    return pl.pallas_call(
        kernel,
        out_shape=jax.ShapeDtypeStruct((2, WIDTH), bf16),
        in_specs=[hbm] * 5,
        out_specs=pl.BlockSpec(memory_space=pltpu.VMEM),
        scratch_shapes=[
            pltpu.VMEM((2, WIDTH), bf16),
            pltpu.SMEM((1,), jnp.int32),
            pltpu.VMEM((4, 128), jnp.int32),
            pltpu.VMEM((2, WIDTH), f32),
            pltpu.VMEM((8, 2, WIDTH), f32),
            pltpu.VMEM((ROWS, WIDTH), f32),
            pltpu.VMEM((2, PLANE, ROWS, WIDTH), bf16),
            pltpu.VMEM((2, ARCHIVE, WIDTH), bf16),
            pltpu.VMEM((WIDTH, 2 * ARCHIVE), bf16),
            pltpu.VMEM((2, ARCHIVE, WIDTH), bf16),
            pltpu.VMEM((2, 8, 128), f32),
            pltpu.VMEM((2, MINE, MINE), bf16),
            pltpu.VMEM((2, GROUP, 2 * ARCHIVE), f32),
            pltpu.VMEM((2, GROUP, 2 * ARCHIVE), bf16),
            pltpu.VMEM((PLANE, ROWS, HALF), bf16),
            pltpu.VMEM((PLANE, ROWS, HALF), bf16),
            pltpu.VMEM((PLANE, ROWS, HALF), bf16),
            pltpu.VMEM((PLANE, ROWS, HALF), bf16),
            pltpu.VMEM((2, PLANE, 2, STATS), f32),
            pltpu.VMEM((2, PLANE, 2, STATS), f32),
            pltpu.VMEM((NZ, 2, WIDTH + STATS), f32),
            pltpu.VMEM((NZ, 2, WIDTH + STATS), f32),
            dma((5,)),
            dma((3,)),
            dma((3,)),
            dma((NZ,)),
            dma((NZ,)),
            dma((PLANE,)),
            dma((PLANE,)),
            dma((PLANE,)),
            dma((PLANE,)),
            dma((2, PLANE)),
            dma((2, PLANE)),
            dma((2, PLANE)),
            dma((2, PLANE)),
            dma((NZ,)),
            dma((NZ,)),
        ],
        compiler_params=pltpu.CompilerParams(
            collective_id=0, has_side_effects=True, vmem_limit_bytes=40 * 2**20
        ),
        name="analog_forecast",
    )(in_hbm(queries), in_hbm(archive_keys), in_hbm(futures), counts, in_hbm(owners.reshape(4, 128)))


def solution(mesh):
    rows = P(("wide", "narrow"), None)
    return jax.shard_map(
        body,
        mesh=mesh,
        in_specs=(rows, rows, rows, P(("wide", "narrow")), P()),
        out_specs=rows,
        check_vma=False,
    )
```

```python
import jax
import jax.numpy as jnp
from jax import lax
from jax.experimental import pallas as pl
from jax.experimental.pallas import tpu as pltpu
from jax.sharding import PartitionSpec as P

MESH = pl.DeviceIdType.MESH

NX, NY, NZ = 4, 4, 8
PLANE = NX * NY
ROWS = 16
MINE = PLANE * ROWS
GROUP = MINE // 2
WIDTH = 1024
HALF = 512
STATS = 128
ARCHIVE = 768
TILE = 256

OFFSETS = (0, 1, 2, 3), (4, 5, 6, 7)

STEPS = sorted(
    [(a, b) for a in range(NX) for b in range(NY) if a or b],
    key=lambda s: -(min(s[0], NX - s[0]) + min(s[1], NY - s[1])),
)

score_scale = 3.0
exponent_factor = score_scale / 32.0 * 1.4426950408889634


def pick(index, values):
    result = jnp.full_like(index, values[0])
    for k in range(1, len(values)):
        result = jnp.where(index == k, values[k], result)
    return result


def natural_row(x, y, z, core, row):
    return x * 128 + z * 16 + core * 8 + y * 2 + row


def kernel(
    queries_hbm,
    keys_hbm,
    futures_hbm,
    counts_hbm,
    owners_hbm,
    out,
    queries,
    counts,
    owners,
    own32,
    zgather,
    gather32,
    gathered,
    keys,
    upright_keys,
    futures,
    limits,
    onehot,
    scores,
    weights,
    low_send,
    low_recv,
    high_send,
    high_recv,
    stat_send,
    stat_recv,
    zpart_send,
    zpart_recv,
    local_sem,
    archive_send,
    archive_recv,
    zg_send,
    zg_recv,
    pg_send,
    pg_recv,
    fw_send,
    fw_recv,
    ps_send,
    ps_recv,
    st_send,
    st_recv,
    zs_send,
    zs_recv,
):
    wide, y = lax.axis_index("wide"), lax.axis_index("narrow")
    x, z, core = wide // 16, (wide // 2) % 8, wide % 2
    plane = x * NY + y

    def device(x, y, z, core):
        return {"wide": (x * NZ + z) * 2 + core, "narrow": y}

    def plane_peer(step):
        other_x, other_y = (x + step[0]) % NX, (y + step[1]) % NY
        return other_x * NY + other_y, device(other_x, other_y, z, core)

    twin = device(x, y, z, 1 - core)

    def remote(src, dst, send, recv, target):
        return pltpu.make_async_remote_copy(
            src_ref=src, dst_ref=dst, send_sem=send, recv_sem=recv, device_id=target, device_id_type=MESH
        )

    loads = [
        pltpu.make_async_copy(src, dst, local_sem.at[k])
        for k, (src, dst) in enumerate(
            [
                (queries_hbm, queries),
                (counts_hbm, counts),
                (owners_hbm, owners),
                (keys_hbm, keys.at[0]),
                (futures_hbm, futures.at[0]),
            ]
        )
    ]
    loads[0].start()
    loads[1].start()

    barrier = pltpu.get_barrier_semaphore()
    for step in (4, 3, 5, 2, 6, 1, 7):
        for side in range(2):
            pl.semaphore_signal(
                barrier, inc=1, device_id=device(x, y, (z + step) % NZ, side), device_id_type=MESH
            )
    for step in STEPS:
        pl.semaphore_signal(barrier, inc=1, device_id=plane_peer(step)[1], device_id_type=MESH)
    pl.semaphore_signal(barrier, inc=1, device_id=twin, device_id_type=MESH)
    for load in loads[2:]:
        load.start()
    loads[0].wait()
    own32[...] = queries[...].astype(jnp.float32)
    loads[1].wait()
    limits[0] = jnp.full((8, 128), counts[0], jnp.int32).astype(jnp.float32)
    pl.semaphore_wait(barrier, 2 * (NZ - 1) + PLANE - 1 + 1)

    zg_sends = []
    for step in (4, 3, 5, 2, 6, 1, 7):
        offset = (NZ - step) % NZ
        side = 0 if offset in OFFSETS[0] else 1
        slot = OFFSETS[side].index(offset) * 2 + core
        copy = remote(
            own32, zgather.at[slot], zg_send.at[step], zg_recv.at[slot], device(x, y, (z + step) % NZ, side)
        )
        copy.start()
        zg_sends.append(copy)
    to_core0 = remote(own32, zgather.at[1], zg_send.at[0], zg_recv.at[1], device(x, y, z, 0))

    @pl.when(core == 1)
    def _():
        to_core0.start()

    @pl.when(core == 0)
    def _():
        zgather[0] = own32[...]

    to_twin = (
        remote(limits.at[0], limits.at[1], archive_send.at[2], archive_recv.at[2], twin),
        remote(keys_hbm, keys.at[1], archive_send.at[0], archive_recv.at[0], twin),
        remote(futures_hbm, futures.at[1], archive_send.at[1], archive_recv.at[1], twin),
    )
    for copy in to_twin:
        copy.start()

    loads[2].wait()
    position = lax.broadcasted_iota(jnp.int32, (1, MINE), 1)
    lane = lax.broadcasted_iota(jnp.int32, (32, 128), 1)
    row = lax.broadcasted_iota(jnp.int32, (32, 128), 0)
    for group in range(2):
        wanted = natural_row(0, row // 8, group * 4 + (row // 2) % 4, core, row % 2)
        for block in range(NX):
            picked = jnp.where(lane == wanted, owners[block : block + 1, :].astype(jnp.float32), 0.0)
            owner = jnp.sum(picked, axis=1, keepdims=True)
            at = group * GROUP + block * 32
            for side in range(2):
                held = natural_row(
                    position // 64,
                    (position // 16) % 4,
                    (z + pick((position // 4) % 4, OFFSETS[side])) % NZ,
                    (position // 2) % 2,
                    position % 2,
                )
                onehot[side, at : at + 32, :] = jnp.where(
                    owner == held.astype(jnp.float32), 1.0, 0.0
                ).astype(jnp.bfloat16)

    def turn_keys(side):
        for tile in range(ARCHIVE // TILE):
            at = side * ARCHIVE + tile * TILE
            upright_keys[:, at : at + TILE] = keys[side, tile * TILE : (tile + 1) * TILE, :].T

    loads[3].wait()
    turn_keys(0)

    def zg_wait(slot):
        remote(own32, zgather.at[slot], zg_send.at[0], zg_recv.at[slot], twin).wait_recv()

    for slot in range(1, 8):
        zg_wait(slot)

    @pl.when(core == 1)
    def _():
        zg_wait(0)

    for slot in range(8):
        gather32[2 * slot : 2 * slot + 2, :] = zgather[slot]
    gathered[core, plane] = gather32[...].astype(jnp.bfloat16)

    pg_sends = []
    for k, step in enumerate(STEPS):
        other, target = plane_peer(step)
        block = gathered.at[core, plane]
        copy = remote(block, block, pg_send.at[k], pg_recv.at[plane], target)
        copy.start()
        pg_sends.append(copy)

    def fw_copy(other):
        block = gathered.at[core, other]
        return remote(block, block, fw_send.at[other], fw_recv.at[other], twin)

    fw_copy(plane).start()
    loads[4].wait()
    for copy in to_twin:
        copy.wait()
    turn_keys(1)
    for step in STEPS:
        other, target = plane_peer(step)
        block = gathered.at[core, other]
        remote(block, block, pg_send.at[0], pg_recv.at[other], target).wait_recv()
        fw_copy(other).start()

    every = gathered[core].reshape(MINE, WIDTH)
    mine = jnp.dot(onehot[core], every, preferred_element_type=jnp.float32)


    def fw_wait(other, carry):
        block = gathered.at[1 - core, other]
        remote(block, block, fw_send.at[other], fw_recv.at[other], twin).wait_recv()
        return carry

    lax.fori_loop(0, PLANE, fw_wait, 0)

    every = gathered[1 - core].reshape(MINE, WIDTH)
    mine = (mine + jnp.dot(onehot[1 - core], every, preferred_element_type=jnp.float32)).astype(jnp.bfloat16)

    column = lax.broadcasted_iota(jnp.int32, (1, TILE), 1).astype(jnp.float32)
    def score(group):
        for side in range(2):
            limit = limits[side, 0:1, 0:1]
            for tile in range(ARCHIVE // TILE):
                at = side * ARCHIVE + tile * TILE
                part = jnp.dot(
                    mine[group * GROUP : (group + 1) * GROUP],
                    upright_keys[:, at : at + TILE],
                    preferred_element_type=jnp.float32,
                )
                if tile > 0:
                    part = jnp.where(column + float(tile * TILE) < limit, part, -1e30)
                scores[group, :, at : at + TILE] = part

    def softmax(group):
        best = None
        for tile in range(2 * ARCHIVE // TILE):
            top = jnp.max(scores[group, :, tile * TILE : (tile + 1) * TILE], axis=1, keepdims=True)
            best = top if best is None else jnp.maximum(best, top)
        total = jnp.zeros((GROUP, 1), jnp.float32)
        for tile in range(2 * ARCHIVE // TILE):
            span = slice(tile * TILE, (tile + 1) * TILE)
            weight = jnp.exp2((scores[group, :, span] - best) * exponent_factor)
            weights[group, :, span] = weight.astype(jnp.bfloat16)
            total = total + jnp.sum(weight, axis=1, keepdims=True)
        return best, total

    here = lax.broadcasted_iota(jnp.int32, (GROUP, STATS), 0) % 8 == lax.broadcasted_iota(jnp.int32, (GROUP, STATS), 1)
    ps_sends, st_sends = [], []
    for group, (send, recv) in enumerate(((low_send, low_recv), (high_send, high_recv))):
        score(group)
        for k, value in enumerate(softmax(group)):
            value = jnp.where(here, value, 0.0).reshape(PLANE, 8, STATS)
            stat_send[group, :, k : k + 1, :] = jnp.sum(value, axis=1, keepdims=True)
        for k, step in enumerate(STEPS):
            other, target = plane_peer(step)
            copy = remote(
                stat_send.at[group, other],
                stat_recv.at[group, plane],
                st_send.at[group, k],
                st_recv.at[group, plane],
                target,
            )
            copy.start()
            st_sends.append(copy)
        stat_recv[group, plane] = stat_send[group, plane]
        halves = []
        for half in range(2):
            span = slice(half * HALF, (half + 1) * HALF)
            sums = None
            for side in range(2):
                term = jnp.dot(
                    weights[group, :, side * ARCHIVE : (side + 1) * ARCHIVE],
                    futures[side, :, span],
                    preferred_element_type=jnp.float32,
                )
                sums = term if sums is None else sums + term
            halves.append(sums.reshape(PLANE, 8, HALF))
        sums = jnp.stack(halves, axis=1).reshape(MINE, HALF)
        send[...] = sums.astype(jnp.bfloat16).reshape(PLANE, ROWS, HALF)
        for k, step in enumerate(STEPS):
            other, target = plane_peer(step)
            copy = remote(send.at[other], recv.at[plane], ps_send.at[group, k], ps_recv.at[group, plane], target)
            copy.start()
            ps_sends.append(copy)
        recv[plane] = send[plane]

    for copy in zg_sends + pg_sends:
        copy.wait_send()

    @pl.when(core == 1)
    def _():
        to_core0.wait_send()

    def fw_sent(other, carry):
        fw_copy(other).wait_send()
        return carry

    lax.fori_loop(0, PLANE, fw_sent, 0)

    at_row = lax.broadcasted_iota(jnp.int32, (8, STATS), 0) == lax.broadcasted_iota(jnp.int32, (8, STATS), 1)

    def upright(value):
        return jnp.sum(jnp.where(at_row, value, 0.0), axis=1, keepdims=True)

    passed_lane = lax.broadcasted_iota(jnp.int32, (1, STATS), 1)
    def zs_copy(group, step):
        other = group * 4 + (z + step) % 4
        return remote(
            zpart_send.at[other],
            zpart_recv.at[z],
            zs_send.at[other],
            zs_recv.at[z],
            device(x, y, other, core),
        )

    for group, (send, recv) in enumerate(((low_send, low_recv), (high_send, high_recv))):
        for step in STEPS:
            other, target = plane_peer(step)
            remote(
                stat_send.at[group, other],
                stat_recv.at[group, other],
                st_send.at[group, 0],
                st_recv.at[group, other],
                target,
            ).wait_recv()
        maxima = [stat_recv[group, k, 0:1, :] for k in range(PLANE)]
        best = maxima[0]
        for k in range(1, PLANE):
            best = jnp.maximum(best, maxima[k])
        scales = [jnp.exp2((m - best) * exponent_factor) for m in maxima]
        total = jnp.zeros((1, STATS), jnp.float32)
        for k in range(PLANE):
            total = total + stat_recv[group, k, 1:2, :] * scales[k]
        passed = jnp.where(passed_lane < 64, upright(best), upright(total))
        def column(other):
            scale = upright(jnp.exp2((stat_recv[group, other, 0:1, :] - best) * exponent_factor))
            return jnp.concatenate([scale, scale], axis=0)

        columns = [column(plane_peer(step)[0]) for step in STEPS]
        sums = recv[plane].astype(jnp.float32) * column(plane)
        for step, scale in zip(STEPS, columns):
            other, target = plane_peer(step)
            remote(send.at[other], recv.at[other], ps_send.at[group, 0], ps_recv.at[group, other], target).wait_recv()
            sums = sums + recv[other].astype(jnp.float32) * scale
        for index in range(4):
            slot = group * 4 + index
            zpart_send[slot, :, :HALF] = sums[2 * index : 2 * index + 2, :]
            zpart_send[slot, :, HALF:WIDTH] = sums[8 + 2 * index : 8 + 2 * index + 2, :]
            zpart_send[slot, :, WIDTH:] = passed[2 * index : 2 * index + 2, :]
        for step in range(3, 0, -1):
            zs_copy(group, step).start()

        @pl.when(z // 4 == group)
        def _():
            zpart_recv[z] = zpart_send[z]

        @pl.when(z // 4 != group)
        def _():
            zs_copy(group, 0).start()

    for copy in st_sends + ps_sends:
        copy.wait_send()

    for step in range(1, NZ):
        other = (z + step) % NZ
        remote(zpart_send.at[0], zpart_recv.at[other], zs_send.at[0], zs_recv.at[other], twin).wait_recv()

    best = zpart_recv[0, :, WIDTH : WIDTH + 1]
    for k in range(1, NZ):
        best = jnp.maximum(best, zpart_recv[k, :, WIDTH : WIDTH + 1])
    sums = jnp.zeros((2, WIDTH), jnp.float32)
    total = jnp.zeros((2, 1), jnp.float32)
    for k in range(NZ):
        stats = zpart_recv[k, :, WIDTH:]
        scale = jnp.exp2((stats[:, 0:1] - best) * exponent_factor)
        sums = sums + zpart_recv[k, :, :WIDTH] * scale
        total = total + stats[:, 64:65] * scale
    analog = sums / total
    norm_factor = lax.rsqrt(jnp.mean(analog * analog, axis=1, keepdims=True) + 1e-06)
    out[...] = (analog * norm_factor).astype(jnp.bfloat16)

    for group in range(2):
        for step in range(1, 4):
            zs_copy(group, step).wait_send()

        @pl.when(z // 4 != group)
        def _():
            zs_copy(group, 0).wait_send()


def in_hbm(array):
    return pltpu.with_memory_space_constraint(array, pltpu.HBM)


def body(queries, archive_keys, futures, counts, owners):
    hbm = pl.BlockSpec(memory_space=pltpu.HBM)
    dma = pltpu.SemaphoreType.DMA
    bf16, f32 = jnp.bfloat16, jnp.float32
    return pl.pallas_call(
        kernel,
        out_shape=jax.ShapeDtypeStruct((2, WIDTH), bf16),
        in_specs=[hbm] * 5,
        out_specs=pl.BlockSpec(memory_space=pltpu.VMEM),
        scratch_shapes=[
            pltpu.VMEM((2, WIDTH), bf16),
            pltpu.SMEM((1,), jnp.int32),
            pltpu.VMEM((4, 128), jnp.int32),
            pltpu.VMEM((2, WIDTH), f32),
            pltpu.VMEM((8, 2, WIDTH), f32),
            pltpu.VMEM((ROWS, WIDTH), f32),
            pltpu.VMEM((2, PLANE, ROWS, WIDTH), bf16),
            pltpu.VMEM((2, ARCHIVE, WIDTH), bf16),
            pltpu.VMEM((WIDTH, 2 * ARCHIVE), bf16),
            pltpu.VMEM((2, ARCHIVE, WIDTH), bf16),
            pltpu.VMEM((2, 8, 128), f32),
            pltpu.VMEM((2, MINE, MINE), bf16),
            pltpu.VMEM((2, GROUP, 2 * ARCHIVE), f32),
            pltpu.VMEM((2, GROUP, 2 * ARCHIVE), bf16),
            pltpu.VMEM((PLANE, ROWS, HALF), bf16),
            pltpu.VMEM((PLANE, ROWS, HALF), bf16),
            pltpu.VMEM((PLANE, ROWS, HALF), bf16),
            pltpu.VMEM((PLANE, ROWS, HALF), bf16),
            pltpu.VMEM((2, PLANE, 2, STATS), f32),
            pltpu.VMEM((2, PLANE, 2, STATS), f32),
            pltpu.VMEM((NZ, 2, WIDTH + STATS), f32),
            pltpu.VMEM((NZ, 2, WIDTH + STATS), f32),
            dma((5,)),
            dma((3,)),
            dma((3,)),
            dma((NZ,)),
            dma((NZ,)),
            dma((PLANE,)),
            dma((PLANE,)),
            dma((PLANE,)),
            dma((PLANE,)),
            dma((2, PLANE)),
            dma((2, PLANE)),
            dma((2, PLANE)),
            dma((2, PLANE)),
            dma((NZ,)),
            dma((NZ,)),
        ],
        compiler_params=pltpu.CompilerParams(
            collective_id=0, has_side_effects=True, vmem_limit_bytes=40 * 2**20
        ),
        name="analog_forecast",
    )(in_hbm(queries), in_hbm(archive_keys), in_hbm(futures), counts, in_hbm(owners.reshape(4, 128)))


def solution(mesh):
    rows = P(("wide", "narrow"), None)
    return jax.shard_map(
        body,
        mesh=mesh,
        in_specs=(rows, rows, rows, P(("wide", "narrow")), P()),
        out_specs=rows,
        check_vma=False,
    )
```

```python
import jax
import jax.numpy as jnp
from jax import lax
from jax.experimental import pallas as pl
from jax.experimental.pallas import tpu as pltpu
from jax.sharding import PartitionSpec as P

MESH = pl.DeviceIdType.MESH

NX, NY, NZ = 4, 4, 8
PLANE = NX * NY
ROWS = 16
MINE = PLANE * ROWS
GROUP = MINE // 2
WIDTH = 1024
HALF = 512
STATS = 128
ARCHIVE = 768
TILE = 256

OFFSETS = (0, 1, 2, 3), (4, 5, 6, 7)

STEPS = sorted(
    [(a, b) for a in range(NX) for b in range(NY) if a or b],
    key=lambda s: -(min(s[0], NX - s[0]) + min(s[1], NY - s[1])),
)

score_scale = 3.0
exponent_factor = score_scale / 32.0 * 1.4426950408889634


def pick(index, values):
    result = jnp.full_like(index, values[0])
    for k in range(1, len(values)):
        result = jnp.where(index == k, values[k], result)
    return result


def natural_row(x, y, z, core, row):
    return x * 128 + z * 16 + core * 8 + y * 2 + row


def kernel(
    queries_hbm,
    keys_hbm,
    futures_hbm,
    counts_hbm,
    owners_hbm,
    out,
    queries,
    counts,
    owners,
    own32,
    zgather,
    gather32,
    gathered,
    keys,
    upright_keys,
    futures,
    limits,
    onehot,
    scores,
    weights,
    low_send,
    low_recv,
    high_send,
    high_recv,
    stat_send,
    stat_recv,
    zpart_send,
    zpart_recv,
    local_sem,
    archive_send,
    archive_recv,
    zg_send,
    zg_recv,
    pg_send,
    pg_recv,
    fw_send,
    fw_recv,
    ps_send,
    ps_recv,
    st_send,
    st_recv,
    zs_send,
    zs_recv,
):
    wide, y = lax.axis_index("wide"), lax.axis_index("narrow")
    x, z, core = wide // 16, (wide // 2) % 8, wide % 2
    plane = x * NY + y

    def device(x, y, z, core):
        return {"wide": (x * NZ + z) * 2 + core, "narrow": y}

    def plane_peer(step):
        other_x, other_y = (x + step[0]) % NX, (y + step[1]) % NY
        return other_x * NY + other_y, device(other_x, other_y, z, core)

    twin = device(x, y, z, 1 - core)

    def remote(src, dst, send, recv, target):
        return pltpu.make_async_remote_copy(
            src_ref=src, dst_ref=dst, send_sem=send, recv_sem=recv, device_id=target, device_id_type=MESH
        )

    loads = [
        pltpu.make_async_copy(src, dst, local_sem.at[k])
        for k, (src, dst) in enumerate(
            [
                (queries_hbm, queries),
                (counts_hbm, counts),
                (owners_hbm, owners),
                (keys_hbm, keys.at[0]),
                (futures_hbm, futures.at[0]),
            ]
        )
    ]
    loads[0].start()
    loads[1].start()

    barrier = pltpu.get_barrier_semaphore()
    for step in (4, 3, 5, 2, 6, 1, 7):
        for side in range(2):
            pl.semaphore_signal(
                barrier, inc=1, device_id=device(x, y, (z + step) % NZ, side), device_id_type=MESH
            )
    for step in STEPS:
        pl.semaphore_signal(barrier, inc=1, device_id=plane_peer(step)[1], device_id_type=MESH)
    pl.semaphore_signal(barrier, inc=1, device_id=twin, device_id_type=MESH)
    for load in loads[2:]:
        load.start()
    loads[0].wait()
    own32[...] = queries[...].astype(jnp.float32)
    loads[1].wait()
    limits[0] = jnp.full((8, 128), counts[0], jnp.int32).astype(jnp.float32)
    pl.semaphore_wait(barrier, 2 * (NZ - 1) + PLANE - 1 + 1)

    zg_sends = []
    for step in (4, 3, 5, 2, 6, 1, 7):
        offset = (NZ - step) % NZ
        side = 0 if offset in OFFSETS[0] else 1
        slot = OFFSETS[side].index(offset) * 2 + core
        copy = remote(
            own32, zgather.at[slot], zg_send.at[step], zg_recv.at[slot], device(x, y, (z + step) % NZ, side)
        )
        copy.start()
        zg_sends.append(copy)
    to_core0 = remote(own32, zgather.at[1], zg_send.at[0], zg_recv.at[1], device(x, y, z, 0))

    @pl.when(core == 1)
    def _():
        to_core0.start()

    @pl.when(core == 0)
    def _():
        zgather[0] = own32[...]

    to_twin = (
        remote(limits.at[0], limits.at[1], archive_send.at[2], archive_recv.at[2], twin),
        remote(keys_hbm, keys.at[1], archive_send.at[0], archive_recv.at[0], twin),
        remote(futures_hbm, futures.at[1], archive_send.at[1], archive_recv.at[1], twin),
    )
    for copy in to_twin:
        copy.start()

    loads[2].wait()
    position = lax.broadcasted_iota(jnp.int32, (1, MINE), 1)
    lane = lax.broadcasted_iota(jnp.int32, (32, 128), 1)
    row = lax.broadcasted_iota(jnp.int32, (32, 128), 0)
    for group in range(2):
        wanted = natural_row(0, row // 8, group * 4 + (row // 2) % 4, core, row % 2)
        for block in range(NX):
            picked = jnp.where(lane == wanted, owners[block : block + 1, :].astype(jnp.float32), 0.0)
            owner = jnp.sum(picked, axis=1, keepdims=True)
            at = group * GROUP + block * 32
            for side in range(2):
                held = natural_row(
                    position // 64,
                    (position // 16) % 4,
                    (z + pick((position // 4) % 4, OFFSETS[side])) % NZ,
                    (position // 2) % 2,
                    position % 2,
                )
                onehot[side, at : at + 32, :] = jnp.where(
                    owner == held.astype(jnp.float32), 1.0, 0.0
                ).astype(jnp.bfloat16)

    def turn_keys(side):
        for tile in range(ARCHIVE // TILE):
            at = side * ARCHIVE + tile * TILE
            upright_keys[:, at : at + TILE] = keys[side, tile * TILE : (tile + 1) * TILE, :].T

    loads[3].wait()
    turn_keys(0)

    def zg_wait(slot):
        remote(own32, zgather.at[slot], zg_send.at[0], zg_recv.at[slot], twin).wait_recv()

    for slot in range(1, 8):
        zg_wait(slot)

    @pl.when(core == 1)
    def _():
        zg_wait(0)

    for slot in range(8):
        gather32[2 * slot : 2 * slot + 2, :] = zgather[slot]
    gathered[core, plane] = gather32[...].astype(jnp.bfloat16)

    pg_sends = []
    for k, step in enumerate(STEPS):
        other, target = plane_peer(step)
        block = gathered.at[core, plane]
        copy = remote(block, block, pg_send.at[k], pg_recv.at[plane], target)
        copy.start()
        pg_sends.append(copy)

    def fw_copy(other):
        block = gathered.at[core, other]
        return remote(block, block, fw_send.at[other], fw_recv.at[other], twin)

    fw_copy(plane).start()
    loads[4].wait()
    for copy in to_twin:
        copy.wait()
    turn_keys(1)
    for step in STEPS:
        other, target = plane_peer(step)
        block = gathered.at[core, other]
        remote(block, block, pg_send.at[0], pg_recv.at[other], target).wait_recv()
        fw_copy(other).start()

    every = gathered[core].reshape(MINE, WIDTH)
    mine = jnp.dot(onehot[core], every, preferred_element_type=jnp.float32)


    def fw_wait(other, carry):
        block = gathered.at[1 - core, other]
        remote(block, block, fw_send.at[other], fw_recv.at[other], twin).wait_recv()
        return carry

    lax.fori_loop(0, PLANE, fw_wait, 0)

    every = gathered[1 - core].reshape(MINE, WIDTH)
    mine = (mine + jnp.dot(onehot[1 - core], every, preferred_element_type=jnp.float32)).astype(jnp.bfloat16)

    column = lax.broadcasted_iota(jnp.int32, (1, TILE), 1).astype(jnp.float32)
    def score(group):
        for side in range(2):
            limit = limits[side, 0:1, 0:1]
            for tile in range(ARCHIVE // TILE):
                at = side * ARCHIVE + tile * TILE
                part = jnp.dot(
                    mine[group * GROUP : (group + 1) * GROUP],
                    upright_keys[:, at : at + TILE],
                    preferred_element_type=jnp.float32,
                )
                if tile > 0:
                    part = jnp.where(column + float(tile * TILE) < limit, part, -1e30)
                scores[group, :, at : at + TILE] = part

    def softmax(group):
        best = None
        for tile in range(2 * ARCHIVE // TILE):
            top = jnp.max(scores[group, :, tile * TILE : (tile + 1) * TILE], axis=1, keepdims=True)
            best = top if best is None else jnp.maximum(best, top)
        total = jnp.zeros((GROUP, 1), jnp.float32)
        for tile in range(2 * ARCHIVE // TILE):
            span = slice(tile * TILE, (tile + 1) * TILE)
            weight = jnp.exp2((scores[group, :, span] - best) * exponent_factor)
            weights[group, :, span] = weight.astype(jnp.bfloat16)
            total = total + jnp.sum(weight, axis=1, keepdims=True)
        return best, total

    here = lax.broadcasted_iota(jnp.int32, (GROUP, STATS), 0) % 8 == lax.broadcasted_iota(jnp.int32, (GROUP, STATS), 1)
    ps_sends, st_sends = [], []
    for group, (send, recv) in enumerate(((low_send, low_recv), (high_send, high_recv))):
        score(group)
        for k, value in enumerate(softmax(group)):
            value = jnp.where(here, value, 0.0).reshape(PLANE, 8, STATS)
            stat_send[group, :, k : k + 1, :] = jnp.sum(value, axis=1, keepdims=True)
        for k, step in enumerate(STEPS):
            other, target = plane_peer(step)
            copy = remote(
                stat_send.at[group, other],
                stat_recv.at[group, plane],
                st_send.at[group, k],
                st_recv.at[group, plane],
                target,
            )
            copy.start()
            st_sends.append(copy)
        stat_recv[group, plane] = stat_send[group, plane]
        halves = []
        for half in range(2):
            span = slice(half * HALF, (half + 1) * HALF)
            sums = None
            for side in range(2):
                term = jnp.dot(
                    weights[group, :, side * ARCHIVE : (side + 1) * ARCHIVE],
                    futures[side, :, span],
                    preferred_element_type=jnp.float32,
                )
                sums = term if sums is None else sums + term
            halves.append(sums.reshape(PLANE, 8, HALF))
        sums = jnp.stack(halves, axis=1).reshape(MINE, HALF)
        send[...] = sums.astype(jnp.bfloat16).reshape(PLANE, ROWS, HALF)
        for k, step in enumerate(STEPS):
            other, target = plane_peer(step)
            copy = remote(send.at[other], recv.at[plane], ps_send.at[group, k], ps_recv.at[group, plane], target)
            copy.start()
            ps_sends.append(copy)
        recv[plane] = send[plane]

    for copy in zg_sends + pg_sends:
        copy.wait_send()

    @pl.when(core == 1)
    def _():
        to_core0.wait_send()

    def fw_sent(other, carry):
        fw_copy(other).wait_send()
        return carry

    lax.fori_loop(0, PLANE, fw_sent, 0)

    at_row = lax.broadcasted_iota(jnp.int32, (8, STATS), 0) == lax.broadcasted_iota(jnp.int32, (8, STATS), 1)

    def upright(value):
        return jnp.sum(jnp.where(at_row, value, 0.0), axis=1, keepdims=True)

    passed_lane = lax.broadcasted_iota(jnp.int32, (1, STATS), 1)
    def zs_copy(group, step):
        other = group * 4 + (z + step) % 4
        return remote(
            zpart_send.at[other],
            zpart_recv.at[z],
            zs_send.at[other],
            zs_recv.at[z],
            device(x, y, other, core),
        )

    for group, (send, recv) in enumerate(((low_send, low_recv), (high_send, high_recv))):
        for step in STEPS:
            other, target = plane_peer(step)
            remote(
                stat_send.at[group, other],
                stat_recv.at[group, other],
                st_send.at[group, 0],
                st_recv.at[group, other],
                target,
            ).wait_recv()
        maxima = [stat_recv[group, k, 0:1, :] for k in range(PLANE)]
        best = maxima[0]
        for k in range(1, PLANE):
            best = jnp.maximum(best, maxima[k])
        scales = [jnp.exp2((m - best) * exponent_factor) for m in maxima]
        total = jnp.zeros((1, STATS), jnp.float32)
        for k in range(PLANE):
            total = total + stat_recv[group, k, 1:2, :] * scales[k]
        scales = [upright(scale) for scale in scales]
        passed = jnp.where(passed_lane < 64, upright(best), upright(total))
        for step in STEPS:
            other, target = plane_peer(step)
            remote(send.at[other], recv.at[other], ps_send.at[group, 0], ps_recv.at[group, other], target).wait_recv()
        sums = jnp.zeros((ROWS, HALF), jnp.float32)
        for k in range(PLANE):
            scale = jnp.concatenate([scales[k], scales[k]], axis=0)
            sums = sums + recv[k].astype(jnp.float32) * scale
        for index in range(4):
            slot = group * 4 + index
            zpart_send[slot, :, :HALF] = sums[2 * index : 2 * index + 2, :]
            zpart_send[slot, :, HALF:WIDTH] = sums[8 + 2 * index : 8 + 2 * index + 2, :]
            zpart_send[slot, :, WIDTH:] = passed[2 * index : 2 * index + 2, :]
        @pl.when(z // 4 != group)
        def _():
            zs_copy(group, 0).start()

        for step in range(3, 0, -1):
            zs_copy(group, step).start()

        @pl.when(z // 4 == group)
        def _():
            zpart_recv[z] = zpart_send[z]

    for copy in st_sends + ps_sends:
        copy.wait_send()

    for step in range(1, NZ):
        other = (z + step) % NZ
        remote(zpart_send.at[0], zpart_recv.at[other], zs_send.at[0], zs_recv.at[other], twin).wait_recv()

    best = zpart_recv[0, :, WIDTH : WIDTH + 1]
    for k in range(1, NZ):
        best = jnp.maximum(best, zpart_recv[k, :, WIDTH : WIDTH + 1])
    sums = jnp.zeros((2, WIDTH), jnp.float32)
    total = jnp.zeros((2, 1), jnp.float32)
    for k in range(NZ):
        stats = zpart_recv[k, :, WIDTH:]
        scale = jnp.exp2((stats[:, 0:1] - best) * exponent_factor)
        sums = sums + zpart_recv[k, :, :WIDTH] * scale
        total = total + stats[:, 64:65] * scale
    analog = sums / total
    norm_factor = lax.rsqrt(jnp.mean(analog * analog, axis=1, keepdims=True) + 1e-06)
    out[...] = (analog * norm_factor).astype(jnp.bfloat16)

    for group in range(2):
        for step in range(1, 4):
            zs_copy(group, step).wait_send()

        @pl.when(z // 4 != group)
        def _():
            zs_copy(group, 0).wait_send()


def in_hbm(array):
    return pltpu.with_memory_space_constraint(array, pltpu.HBM)


def body(queries, archive_keys, futures, counts, owners):
    hbm = pl.BlockSpec(memory_space=pltpu.HBM)
    dma = pltpu.SemaphoreType.DMA
    bf16, f32 = jnp.bfloat16, jnp.float32
    return pl.pallas_call(
        kernel,
        out_shape=jax.ShapeDtypeStruct((2, WIDTH), bf16),
        in_specs=[hbm] * 5,
        out_specs=pl.BlockSpec(memory_space=pltpu.VMEM),
        scratch_shapes=[
            pltpu.VMEM((2, WIDTH), bf16),
            pltpu.SMEM((1,), jnp.int32),
            pltpu.VMEM((4, 128), jnp.int32),
            pltpu.VMEM((2, WIDTH), f32),
            pltpu.VMEM((8, 2, WIDTH), f32),
            pltpu.VMEM((ROWS, WIDTH), f32),
            pltpu.VMEM((2, PLANE, ROWS, WIDTH), bf16),
            pltpu.VMEM((2, ARCHIVE, WIDTH), bf16),
            pltpu.VMEM((WIDTH, 2 * ARCHIVE), bf16),
            pltpu.VMEM((2, ARCHIVE, WIDTH), bf16),
            pltpu.VMEM((2, 8, 128), f32),
            pltpu.VMEM((2, MINE, MINE), bf16),
            pltpu.VMEM((2, GROUP, 2 * ARCHIVE), f32),
            pltpu.VMEM((2, GROUP, 2 * ARCHIVE), bf16),
            pltpu.VMEM((PLANE, ROWS, HALF), bf16),
            pltpu.VMEM((PLANE, ROWS, HALF), bf16),
            pltpu.VMEM((PLANE, ROWS, HALF), bf16),
            pltpu.VMEM((PLANE, ROWS, HALF), bf16),
            pltpu.VMEM((2, PLANE, 2, STATS), f32),
            pltpu.VMEM((2, PLANE, 2, STATS), f32),
            pltpu.VMEM((NZ, 2, WIDTH + STATS), f32),
            pltpu.VMEM((NZ, 2, WIDTH + STATS), f32),
            dma((5,)),
            dma((3,)),
            dma((3,)),
            dma((NZ,)),
            dma((NZ,)),
            dma((PLANE,)),
            dma((PLANE,)),
            dma((PLANE,)),
            dma((PLANE,)),
            dma((2, PLANE)),
            dma((2, PLANE)),
            dma((2, PLANE)),
            dma((2, PLANE)),
            dma((NZ,)),
            dma((NZ,)),
        ],
        compiler_params=pltpu.CompilerParams(
            collective_id=0, has_side_effects=True, vmem_limit_bytes=40 * 2**20
        ),
        name="analog_forecast",
    )(in_hbm(queries), in_hbm(archive_keys), in_hbm(futures), counts, in_hbm(owners.reshape(4, 128)))


def solution(mesh):
    rows = P(("wide", "narrow"), None)
    return jax.shard_map(
        body,
        mesh=mesh,
        in_specs=(rows, rows, rows, P(("wide", "narrow")), P()),
        out_specs=rows,
        check_vma=False,
    )
```
